256 devices in a mesh: peer: 16 (over z_lo, x, core), fsdp: 16 (over y, z_hi).
Axes of the slice: x: 4, y: 4, z: 8 (z_hi: 4, z_lo: 2; z = z_hi * 2 + z_lo), core: 2. Of those that a mesh axis runs over, the one named last changes fastest.
Arguments:
- tokens: bfloat16 [16, 2048, 2048], P('peer', 'fsdp'), may hold values from -6 to 6
- gate_weight: bfloat16 [16, 5632, 2048], P('peer', 'fsdp'), may hold values from -6 to 6
- up_weight: bfloat16 [16, 5632, 2048], P('peer', 'fsdp'), may hold values from -6 to 6
- down_weight: bfloat16 [16, 5632, 2048], P('peer', 'fsdp'), may hold values from -6 to 6
- cotangent: bfloat16 [16, 2048, 2048], P('peer', 'fsdp'), may hold values from -6 to 6
Outputs:
- new_gate: bfloat16 [16, 5632, 2048], P('peer', 'fsdp')
- new_up: bfloat16 [16, 5632, 2048], P('peer', 'fsdp')
The draws below stay inside these ranges and needn't reach their ends.
All inputs are finite; a program needn't handle non-finite values.
Results may differ from the reference program's by a relative error of at most 0.0054.
Values may be sent and summed in bfloat16 or wider, within the bound.
No kernel may reach another device: no remote copies, remote signals or barrier semaphores. Data moves between devices by JAX's collectives and lax.ppermute only.
A program may use at most 128 MiB of HBM per device.

```python
import jax
import jax.numpy as jnp
from jax import lax

D = 2048
FF = 5632
HOP = 2
GROUPS = 16
TOK_GROUP = 2048


def block_levels(stream_key, extent, pieces, smallest, top_value):
    def one(position, blocks):
        heights = jax.random.uniform(jax.random.fold_in(jax.random.fold_in(stream_key, 6), position), (blocks,), jnp.float32, smallest / len(pieces), top_value / len(pieces))
        return jnp.repeat(jnp.exp(heights), extent[position] // blocks).reshape((-1,) + (1,) * (len(extent) - position - 1))

    level = one(*pieces[0])
    for cut in pieces[1:]:
        level = level * one(*cut)
    return level


def scatter_about(own_key, dims, scale, reach, pieces=(), held_as=jnp.bfloat16):
    loudness = block_levels(own_key, dims, pieces, -0.22, 0.18) if pieces else 1.0
    values = jax.random.normal(own_key, dims, jnp.float32) * scale * loudness
    return jnp.minimum(jnp.maximum(values, -reach), reach).astype(held_as)


def setup_inputs(seed: int = 0) -> dict:
    key_of = jax.random.split(jax.random.key(seed), 6)
    return {
        "tokens": scatter_about(key_of[0], (GROUPS, TOK_GROUP, D), 1.0, 6.0, ((0, 16), (1, 16))),
        "gate_weight": scatter_about(key_of[1], (GROUPS, FF, D), 1.0, 6.0, ((0, 16), (1, 16))),
        "up_weight": scatter_about(key_of[2], (GROUPS, FF, D), 1.0, 6.0, ((0, 16), (1, 16))),
        "down_weight": scatter_about(key_of[3], (GROUPS, FF, D), 1.0, 6.0, ((0, 16), (1, 16))),
        "cotangent": scatter_about(key_of[4], (GROUPS, TOK_GROUP, D), 1.0, 6.0, ((0, 16), (1, 16))),
    }


rate_value = 1.0


def group_step(operands):
    tokens_in, gate_in, up_in, down_in, cotangent_in = operands
    gate = jnp.dot(tokens_in, gate_in.T, preferred_element_type=jnp.float32) * (D ** -0.5)
    upper = jnp.dot(tokens_in, up_in.T, preferred_element_type=jnp.float32) * (D ** -0.5)
    dhidden = jnp.dot(cotangent_in, down_in.T, preferred_element_type=jnp.float32) * (FF ** -0.5)
    sigma = jax.nn.sigmoid(gate)
    dgate = (dhidden * upper * sigma * (1.0 + gate * (1.0 - sigma))).astype(jnp.bfloat16)
    dupper = (dhidden * gate * sigma).astype(jnp.bfloat16)
    grad_gate = jnp.dot(dgate.T, tokens_in, preferred_element_type=jnp.float32) * (D ** -0.5)
    grad_upper = jnp.dot(dupper.T, tokens_in, preferred_element_type=jnp.float32) * (D ** -0.5)
    stepped_gate = (gate_in.astype(jnp.float32) - rate_value * grad_gate).astype(jnp.bfloat16)
    stepped_upper = (up_in.astype(jnp.float32) - rate_value * grad_upper).astype(jnp.bfloat16)
    return stepped_gate, stepped_upper


def reference(tokens, gate_weight, up_weight, down_weight, cotangent):
    stepped_gate, stepped_upper = lax.map(group_step, (tokens, gate_weight, up_weight, down_weight, cotangent))
    partner_gate = jnp.roll(stepped_gate, HOP, axis=0)
    partner_upper = jnp.roll(stepped_upper, HOP, axis=0)
    new_gate = ((stepped_gate.astype(jnp.float32) + partner_gate.astype(jnp.float32)) * 0.5).astype(jnp.bfloat16)
    new_up = ((stepped_upper.astype(jnp.float32) + partner_upper.astype(jnp.float32)) * 0.5).astype(jnp.bfloat16)
    return new_gate, new_up
```

```python
import functools

import jax
import jax.numpy as jnp
from jax import lax
from jax.experimental import pallas as pl
from jax.experimental.pallas import tpu as pltpu
from jax.sharding import PartitionSpec as P

D = 2048
FF = 5632
HOP = 2
ROWS = 352
SHARE = 128
FIRST = 48
SECOND = 16
TILE = 256

rate_value = 1.0

AXES = ("peer", "fsdp")


def device_index(z_lo, x, core, y, z_hi):
    return ((z_lo * 4 + x) * 2 + core) * 16 + y * 4 + z_hi


def shifted(block, y=0, z=0):
    pairs = []
    for z_lo in range(2):
        for x in range(4):
            for core in range(2):
                for at_y in range(4):
                    for at_z in range(4):
                        pairs.append(
                            (
                                device_index(z_lo, x, core, at_y, at_z),
                                device_index(z_lo, x, core, (at_y + y) % 4, (at_z + z) % 4),
                            )
                        )
    return lax.ppermute(block, AXES, pairs)


def to_partner(block):
    peers = lax.axis_size("peer")
    return lax.ppermute(block, "peer", [(i, (i + HOP) % peers) for i in range(peers)])


def contract_last(left, right):
    return lax.dot_general(
        left, right, (((1,), (1,)), ((), ())), preferred_element_type=jnp.float32
    )


def sub_blocks(piece):
    lead = piece.shape[:-3]
    found = [()]
    for size in lead:
        found = [index + (i,) for index in found for i in range(size)]
    return found


def grad_kernel(count, first, last, *refs):
    pieces = refs[:count]
    gate_hbm, up_hbm, down_hbm = refs[count : count + 3]
    refs = refs[count + 3 :]
    if not first:
        sum_in, refs = refs[0], refs[1:]
    if last:
        gate_out, up_out, refs = refs[0], refs[1], refs[2:]
    else:
        sum_out, refs = refs[0], refs[1:]
    tokens, cots, weights, down, slopes, total, sems = refs
    amount = tokens.shape[0]
    steps = amount // TILE
    columns = D // TILE

    slot = 0
    loads = []

    def begin(source, target):
        nonlocal slot
        copy = pltpu.make_async_copy(source, target, sems.at[slot])
        slot += 1
        copy.start()
        return copy

    loads.append(begin(gate_hbm, weights.at[pl.ds(0, ROWS)]))
    loads.append(begin(up_hbm, weights.at[pl.ds(ROWS, ROWS)]))
    offset = 0
    for piece in pieces:
        size = piece.shape[-2]
        for index in sub_blocks(piece):
            loads.append(begin(piece.at[index + (0,)], tokens.at[pl.ds(offset, size)]))
            loads.append(begin(piece.at[index + (1,)], cots.at[pl.ds(offset, size)]))
            offset += size
    loads.append(begin(down_hbm, down))
    sums = []
    if not first:
        for column in range(columns):
            part = pl.ds(column * TILE, TILE)
            sums.append(begin(sum_in.at[:, part], total.at[:, part]))
    for copy in loads:
        copy.wait()

    def one_tile(step, carry):
        rows = pl.ds(pl.multiple_of(step * TILE, TILE), TILE)
        both = contract_last(weights[...], tokens[rows, :]) * D ** (-0.5)
        gate, up = both[:ROWS], both[ROWS:]
        dhidden = contract_last(down[...], cots[rows, :]) * FF ** (-0.5)
        sigma = jax.nn.sigmoid(gate)
        slopes[:ROWS, rows] = (dhidden * up * sigma * (1.0 + gate * (1.0 - sigma))).astype(
            jnp.bfloat16
        )
        slopes[ROWS:, rows] = (dhidden * gate * sigma).astype(jnp.bfloat16)
        return carry

    lax.fori_loop(0, steps, one_tile, 0)

    stores = []
    for column in range(columns):
        part = pl.ds(column * TILE, TILE)
        grad = jnp.dot(slopes[...], tokens[:, part], preferred_element_type=jnp.float32)
        if not first:
            sums[column].wait()
            grad = total[:, part] + grad
        if last:
            stepped = (
                weights[:, part].astype(jnp.float32) - rate_value * (grad * D ** (-0.5))
            ).astype(jnp.bfloat16)
            gate_out[:, part] = stepped[:ROWS]
            up_out[:, part] = stepped[ROWS:]
        else:
            total[:, part] = grad
            stores.append(begin(total.at[:, part], sum_out.at[:, part]))
    for copy in stores:
        copy.wait()


def add_grads(pieces, gate, up, down, so_far=None, last=False):
    amount = 0
    copies = 3 + 2 * (D // TILE)
    for piece in pieces:
        blocks = len(sub_blocks(piece))
        amount += blocks * piece.shape[-2]
        copies += 2 * blocks
    first = so_far is None
    operands = list(pieces) + [gate, up, down] + ([] if first else [so_far])
    anywhere = pl.BlockSpec(memory_space=pl.ANY)
    whole = pl.BlockSpec(memory_space=pltpu.VMEM)
    if last:
        out_shape = (jax.ShapeDtypeStruct((ROWS, D), jnp.bfloat16),) * 2
        out_specs = (whole, whole)
    else:
        out_shape = jax.ShapeDtypeStruct((2 * ROWS, D), jnp.float32)
        out_specs = anywhere
    return pl.pallas_call(
        functools.partial(grad_kernel, len(pieces), first, last),
        out_shape=out_shape,
        in_specs=[anywhere] * len(operands),
        out_specs=out_specs,
        scratch_shapes=[
            pltpu.VMEM((amount, D), jnp.bfloat16),
            pltpu.VMEM((amount, D), jnp.bfloat16),
            pltpu.VMEM((2 * ROWS, D), jnp.bfloat16),
            pltpu.VMEM((ROWS, D), jnp.bfloat16),
            pltpu.VMEM((2 * ROWS, amount), jnp.bfloat16),
            pltpu.VMEM((2 * ROWS, D), jnp.float32),
            pltpu.SemaphoreType.DMA((copies,)),
        ],
        compiler_params=pltpu.CompilerParams(vmem_limit_bytes=40 * 1024 * 1024),
        cost_estimate=pl.CostEstimate(
            flops=10 * amount * D * ROWS, bytes_accessed=20 * 1024 * 1024, transcendentals=amount * ROWS
        ),
    )(*operands)


def averaged(mine, theirs):
    return ((mine.astype(jnp.float32) + theirs.astype(jnp.float32)) * 0.5).astype(jnp.bfloat16)


def body(tokens, gate_weight, up_weight, down_weight, cotangent):
    gate, up, down = gate_weight[0], up_weight[0], down_weight[0]
    grads = functools.partial(add_grads, gate=gate, up=up, down=down)

    along_z = jnp.stack(
        [
            jnp.stack([tokens[0, h * FIRST : (h + 1) * FIRST], cotangent[0, h * FIRST : (h + 1) * FIRST]])
            for h in range(2)
        ]
    )
    start = 2 * FIRST
    along_y = jnp.stack(
        [
            jnp.stack(
                [
                    tokens[0, start + h * SECOND : start + (h + 1) * SECOND],
                    cotangent[0, start + h * SECOND : start + (h + 1) * SECOND],
                ]
            )
            for h in range(2)
        ]
    )
    own = jnp.concatenate([along_z, along_y], axis=2)

    z_up = shifted(along_z, z=1)
    z_down = shifted(along_z, z=-1)
    y_up = shifted(own, y=1)
    y_down = shifted(own, y=-1)
    far_y = (shifted(y_up[0], y=1), shifted(y_down[1], y=-1))
    far_z = (shifted(z_up[0], z=1), shifted(z_down[1], z=-1))

    near = jnp.stack([z_up, z_down])
    near_up = shifted(near, y=1)
    near_down = shifted(near, y=-1)
    near_far = (shifted(near_up[0], y=1), shifted(near_down[1], y=-1))

    row = jnp.stack(
        [along_y, y_up[:, :, FIRST:], y_down[:, :, FIRST:], jnp.stack([part[:, FIRST:] for part in far_y])]
    )
    row_up = shifted(row, z=1)
    row_down = shifted(row, z=-1)
    row_far = (shifted(row_up[:2], z=1), shifted(row_down[2:], z=-1))

    opposite = jnp.stack(far_z)
    opposite_up = shifted(opposite, y=1)
    opposite_down = shifted(opposite, y=-1)
    opposite_far = (shifted(opposite_up[0], y=1), shifted(opposite_down[1], y=-1))

    total = grads([own, y_up, y_down, *far_y])
    total = grads([near, *far_z, near_up, near_down, near_far[0]], so_far=total)
    total = grads([near_far[1], opposite_up, opposite_down, *opposite_far, row_up], so_far=total)
    stepped_gate, stepped_up = grads([row_down, *row_far], so_far=total, last=True)

    partner_gate = to_partner(stepped_gate)
    partner_up = to_partner(stepped_up)
    return (averaged(stepped_gate, partner_gate)[None], averaged(stepped_up, partner_up)[None])


def solution(mesh):
    spec = P("peer", "fsdp", None)
    return jax.shard_map(
        body,
        mesh=mesh,
        in_specs=(spec,) * 5,
        out_specs=(spec, spec),
        check_vma=False,
    )
```

```python
import functools

import jax
import jax.numpy as jnp
from jax import lax
from jax.experimental import pallas as pl
from jax.experimental.pallas import tpu as pltpu
from jax.sharding import PartitionSpec as P

D = 2048
FF = 5632
HOP = 2
ROWS = 352
FIRST = 112
HALF = 64
TILE = 256

rate_value = 1.0

AXES = ("peer", "fsdp")


def device_index(z_lo, x, core, y, z_hi):
    return ((z_lo * 4 + x) * 2 + core) * 16 + y * 4 + z_hi


def places(cores):
    return [
        (z_lo, x, core, y, z_hi)
        for z_lo in range(2)
        for x in range(4)
        for core in cores
        for y in range(4)
        for z_hi in range(4)
    ]


def shifted(block, cores, y=0, z=0):
    pairs = [
        (
            device_index(z_lo, x, core, at_y, at_z),
            device_index(z_lo, x, core, (at_y + y) % 4, (at_z + z) % 4),
        )
        for z_lo, x, core, at_y, at_z in places(cores)
    ]
    return lax.ppermute(block, AXES, pairs)


def to_partner(block, cores):
    peers = lax.axis_size("peer")
    pairs = [(i, (i + HOP) % peers) for i in range(peers) if i % 2 in cores]
    return lax.ppermute(block, "peer", pairs)


def to_other_core(block):
    peers = lax.axis_size("peer")
    return lax.ppermute(block, "peer", [(i, i + 1) for i in range(0, peers, 2)])


def contract_last(left, right):
    return lax.dot_general(
        left, right, (((1,), (1,)), ((), ())), preferred_element_type=jnp.float32
    )


def sub_blocks(piece):
    found = [()]
    for size in piece.shape[:-3]:
        found = [index + (i,) for index in found for i in range(size)]
    return found


def add_up(count, first, last, amount, pieces, weights, down, sum_in, outs, tokens, cots, slopes, sems):
    loads = []

    def begin(source, target):
        copy = pltpu.make_async_copy(source, target, sems.at[len(loads)])
        copy.start()
        loads.append(copy)

    offset = 0
    ends = []
    for piece in pieces:
        size = piece.shape[-2]
        for index in sub_blocks(piece):
            begin(piece.at[index + (0,)], tokens.at[pl.ds(offset, size)])
            begin(piece.at[index + (1,)], cots.at[pl.ds(offset, size)])
            offset += size
            ends += [offset, offset]
    padded = tokens.shape[0]
    if padded > offset:
        tokens[offset:, :] = jnp.zeros((padded - offset, D), jnp.bfloat16)
        cots[offset:, :] = jnp.zeros((padded - offset, D), jnp.bfloat16)

    waited = 0
    for start in range(0, padded, TILE):
        size = min(TILE, padded - start)
        while waited < len(loads) and (waited == 0 or ends[waited - 1] < start + size):
            loads[waited].wait()
            loads[waited + 1].wait()
            waited += 2
        rows = pl.ds(start, size)
        both = contract_last(weights[...], tokens[rows, :]) * D ** (-0.5)
        gate, up = both[:ROWS], both[ROWS:]
        dhidden = contract_last(down[...], cots[rows, :]) * FF ** (-0.5)
        sigma = jax.nn.sigmoid(gate)
        slopes[:ROWS, rows] = (dhidden * up * sigma * (1.0 + gate * (1.0 - sigma))).astype(
            jnp.bfloat16
        )
        slopes[ROWS:, rows] = (dhidden * gate * sigma).astype(jnp.bfloat16)

    for column in range(D // TILE):
        part = pl.ds(column * TILE, TILE)
        grad = jnp.dot(slopes[...], tokens[:, part], preferred_element_type=jnp.float32)
        if not first:
            grad = sum_in[:, part] + grad
        if last:
            stepped = (
                weights[:, part].astype(jnp.float32) - rate_value * (grad * D ** (-0.5))
            ).astype(jnp.bfloat16)
            outs[0][:, part] = stepped[:ROWS]
            outs[1][:, part] = stepped[ROWS:]
        else:
            outs[0][:, part] = grad


def grad_kernel(count, first, last, amount, *refs):
    active, refs = refs[0], refs[1:]
    pieces = refs[:count]
    weights, down = refs[count : count + 2]
    refs = refs[count + 2 :]
    sum_in = None
    if not first:
        sum_in, refs = refs[0], refs[1:]
    wide = 2 if last else 1
    outs, scratch = refs[:wide], refs[wide:]

    @pl.when(active[0] == 1)
    def _():
        add_up(count, first, last, amount, pieces, weights, down, sum_in, outs, *scratch)


def add_grads(pieces, active, weights, down, so_far=None, last=False):
    amount = 0
    copies = 0
    for piece in pieces:
        blocks = len(sub_blocks(piece))
        amount += blocks * piece.shape[-2]
        copies += 2 * blocks
    padded = -(-amount // 128) * 128
    first = so_far is None
    operands = [active] + list(pieces) + [weights, down] + ([] if first else [so_far])
    whole = pl.BlockSpec(memory_space=pltpu.VMEM)
    anywhere = pl.BlockSpec(memory_space=pl.ANY)
    in_specs = [pl.BlockSpec(memory_space=pltpu.SMEM)]
    in_specs += [anywhere] * len(pieces) + [whole] * (len(operands) - 1 - len(pieces))
    if last:
        out_shape = (jax.ShapeDtypeStruct((ROWS, D), jnp.bfloat16),) * 2
        out_specs = (whole, whole)
    else:
        out_shape = jax.ShapeDtypeStruct((2 * ROWS, D), jnp.float32)
        out_specs = whole
    return pl.pallas_call(
        functools.partial(grad_kernel, len(pieces), first, last, amount),
        out_shape=out_shape,
        in_specs=in_specs,
        out_specs=out_specs,
        input_output_aliases={} if first or last else {len(operands) - 1: 0},
        scratch_shapes=[
            pltpu.VMEM((padded, D), jnp.bfloat16),
            pltpu.VMEM((padded, D), jnp.bfloat16),
            pltpu.VMEM((2 * ROWS, padded), jnp.bfloat16),
            pltpu.SemaphoreType.DMA((copies,)),
        ],
        compiler_params=pltpu.CompilerParams(vmem_limit_bytes=24 * 1024 * 1024),
        cost_estimate=pl.CostEstimate(
            flops=10 * amount * D * ROWS, bytes_accessed=amount * D, transcendentals=0
        ),
    )(*operands)


def averaged(mine, theirs):
    return ((mine.astype(jnp.float32) + theirs.astype(jnp.float32)) * 0.5).astype(jnp.bfloat16)


def group_step(own, weights, down, active, cores):
    grads = functools.partial(add_grads, active=active, weights=weights, down=down)
    move = functools.partial(shifted, cores=cores)
    hold = lax.optimization_barrier
    join = functools.partial(jnp.concatenate, axis=1)

    y_up, y_down = move(own, y=1), move(own, y=-1)
    along_z = own[:, :FIRST]
    z_up, z_down = move(along_z, z=1), move(along_z, z=-1)
    far_y = (move(y_up[:, :HALF], y=1), move(y_down[:, HALF:], y=-1))
    far_z = (move(z_up[:, :HALF], z=1), move(z_down[:, HALF:], z=-1))

    *far_y, z_up, z_down = hold((*far_y, z_up, z_down))
    near = jnp.stack([z_up, z_down])
    row = join([part[:, FIRST:] for part in (own, y_up, y_down)] + [far_y[1][:, FIRST - HALF :]])
    near, row = hold((near, row))
    near_up, near_down = move(near, y=1), move(near, y=-1)
    *far_z, row = hold((*far_z, row))
    told = to_other_core(far_z[0][0, :16]) if 0 in cores else row[0, :16]
    row_up, row_down = move(row, z=1), move(row, z=-1)
    own, row, told = hold((own, row, told))
    total = grads([own, y_up, y_down, *far_y, near, *far_z])

    opposite = join(far_z)
    near_up, near_down, row_up, row_down, total = hold((near_up, near_down, row_up, row_down, total))
    last_up = move(join([near_up[0], opposite]), y=1)
    last_down = move(join([near_down[1], opposite]), y=-1)
    wide = row.shape[1] // 2
    row_far = (move(row_up[:, :wide], z=1), move(row_down[:, wide:], z=-1))
    total = grads([near_up, near_down, row_up, row_down], so_far=total)
    last_up, last_down, total = hold((last_up, last_down, total))
    opposite_far = (
        move(last_up[:, FIRST : FIRST + HALF], y=1),
        move(last_down[:, FIRST + HALF :], y=-1),
    )
    total = grads([last_up, last_down, *row_far], so_far=total)
    stepped = grads(opposite_far, so_far=total, last=True)
    return stepped, told


def body(tokens, gate_weight, up_weight, down_weight, cotangent):
    hold = lax.optimization_barrier
    weights = jnp.concatenate([gate_weight[0], up_weight[0]])
    down = down_weight[0]
    core = lax.axis_index("peer") % 2

    own = jnp.stack([tokens[0], cotangent[0]])

    active = (core == 0).astype(jnp.int32).reshape(1)
    (gate, up), told = group_step(own, weights, down, active, (0,))
    first_gate = averaged(gate, to_partner(gate, (0,)))
    first_up = averaged(up, to_partner(up, (0,)))

    own, told, first_gate, first_up = hold((own, told, first_gate, first_up))
    active = (core == 1).astype(jnp.int32).reshape(1)
    (gate, up), _ = group_step(own, weights, down, active, (1,))
    second_gate = averaged(gate, to_partner(gate, (1,)))
    second_up = averaged(up, to_partner(up, (1,)))
    mine = (core == 0) & (told[0, 0] < 128.0)
    return (
        jnp.where(mine, first_gate, second_gate)[None],
        jnp.where(mine, first_up, second_up)[None],
    )


def solution(mesh):
    spec = P("peer", "fsdp", None)
    return jax.shard_map(
        body,
        mesh=mesh,
        in_specs=(spec,) * 5,
        out_specs=(spec, spec),
        check_vma=False,
    )
```

```python
import functools

import jax
import jax.numpy as jnp
from jax import lax
from jax.experimental import pallas as pl
from jax.experimental.pallas import tpu as pltpu
from jax.sharding import PartitionSpec as P

D = 2048
FF = 5632
HOP = 2
ROWS = 352
FIRST = 112
HALF = 64
TILE = 256

rate_value = 1.0

AXES = ("peer", "fsdp")


def device_index(z_lo, x, core, y, z_hi):
    return ((z_lo * 4 + x) * 2 + core) * 16 + y * 4 + z_hi


def shifted(block, y=0, z=0):
    pairs = [
        (
            device_index(z_lo, x, core, at_y, at_z),
            device_index(z_lo, x, core, (at_y + y) % 4, (at_z + z) % 4),
        )
        for z_lo in range(2)
        for x in range(4)
        for core in range(2)
        for at_y in range(4)
        for at_z in range(4)
    ]
    return lax.ppermute(block, AXES, pairs)


def from_below(block):
    peers = lax.axis_size("peer")
    return lax.ppermute(block, "peer", [(i, (i + HOP) % peers) for i in range(1, peers, 2)])


def across(block):
    peers = lax.axis_size("peer")
    pairs = [(i, (i + (HOP if i % 2 == 0 else -HOP)) % peers) for i in range(peers)]
    return lax.ppermute(block, "peer", pairs)


def contract_last(left, right):
    return lax.dot_general(
        left, right, (((1,), (1,)), ((), ())), preferred_element_type=jnp.float32
    )


def sub_blocks(piece):
    found = [()]
    for size in piece.shape[:-3]:
        found = [index + (i,) for index in found for i in range(size)]
    return found


def add_up(count, first, last, amount, pieces, weights, down, sum_in, outs, tokens, cots, slopes, sems):
    loads = []

    def begin(source, target):
        copy = pltpu.make_async_copy(source, target, sems.at[len(loads)])
        copy.start()
        loads.append(copy)

    offset = 0
    ends = []
    for piece in pieces:
        size = piece.shape[-2]
        for index in sub_blocks(piece):
            begin(piece.at[index + (0,)], tokens.at[pl.ds(offset, size)])
            begin(piece.at[index + (1,)], cots.at[pl.ds(offset, size)])
            offset += size
            ends += [offset, offset]
    padded = tokens.shape[0]
    if padded > offset:
        tokens[offset:, :] = jnp.zeros((padded - offset, D), jnp.bfloat16)
        cots[offset:, :] = jnp.zeros((padded - offset, D), jnp.bfloat16)

    waited = 0
    for start in range(0, padded, TILE):
        size = min(TILE, padded - start)
        while waited < len(loads) and (waited == 0 or ends[waited - 1] < start + size):
            loads[waited].wait()
            loads[waited + 1].wait()
            waited += 2
        rows = pl.ds(start, size)
        both = contract_last(weights[...], tokens[rows, :]) * D ** (-0.5)
        gate, up = both[:ROWS], both[ROWS:]
        dhidden = contract_last(down[...], cots[rows, :]) * FF ** (-0.5)
        sigma = jax.nn.sigmoid(gate)
        slopes[:ROWS, rows] = (dhidden * up * sigma * (1.0 + gate * (1.0 - sigma))).astype(
            jnp.bfloat16
        )
        slopes[ROWS:, rows] = (dhidden * gate * sigma).astype(jnp.bfloat16)

    for column in range(D // TILE):
        part = pl.ds(column * TILE, TILE)
        grad = jnp.dot(slopes[...], tokens[:, part], preferred_element_type=jnp.float32)
        if not first:
            grad = sum_in[:, part] + grad
        if last:
            stepped = (
                weights[:, part].astype(jnp.float32) - rate_value * (grad * D ** (-0.5))
            ).astype(jnp.bfloat16)
            outs[0][:, part] = stepped[:ROWS]
            outs[1][:, part] = stepped[ROWS:]
        else:
            outs[0][:, part] = grad


def grad_kernel(count, first, last, amount, *refs):
    pieces = refs[:count]
    weights, down = refs[count : count + 2]
    refs = refs[count + 2 :]
    sum_in = None
    if not first:
        sum_in, refs = refs[0], refs[1:]
    wide = 2 if last else 1
    outs, scratch = refs[:wide], refs[wide:]
    add_up(count, first, last, amount, pieces, weights, down, sum_in, outs, *scratch)


def add_grads(pieces, weights, down, so_far=None, last=False):
    amount = 0
    copies = 0
    for piece in pieces:
        blocks = len(sub_blocks(piece))
        amount += blocks * piece.shape[-2]
        copies += 2 * blocks
    padded = -(-amount // 128) * 128
    first = so_far is None
    operands = list(pieces) + [weights, down] + ([] if first else [so_far])
    whole = pl.BlockSpec(memory_space=pltpu.VMEM)
    anywhere = pl.BlockSpec(memory_space=pl.ANY)
    in_specs = [anywhere] * len(pieces) + [whole] * (len(operands) - len(pieces))
    if last:
        out_shape = (jax.ShapeDtypeStruct((ROWS, D), jnp.bfloat16),) * 2
        out_specs = (whole, whole)
    else:
        out_shape = jax.ShapeDtypeStruct((2 * ROWS, D), jnp.float32)
        out_specs = whole
    return pl.pallas_call(
        functools.partial(grad_kernel, len(pieces), first, last, amount),
        out_shape=out_shape,
        in_specs=in_specs,
        out_specs=out_specs,
        input_output_aliases={} if first or last else {len(operands) - 1: 0},
        scratch_shapes=[
            pltpu.VMEM((padded, D), jnp.bfloat16),
            pltpu.VMEM((padded, D), jnp.bfloat16),
            pltpu.VMEM((2 * ROWS, padded), jnp.bfloat16),
            pltpu.SemaphoreType.DMA((copies,)),
        ],
        compiler_params=pltpu.CompilerParams(vmem_limit_bytes=24 * 1024 * 1024),
        cost_estimate=pl.CostEstimate(
            flops=10 * amount * D * ROWS, bytes_accessed=amount * D, transcendentals=0
        ),
    )(*operands)


def averaged(mine, theirs):
    return ((mine.astype(jnp.float32) + theirs.astype(jnp.float32)) * 0.5).astype(jnp.bfloat16)


def body(tokens, gate_weight, up_weight, down_weight, cotangent):
    move = shifted
    hold = lax.optimization_barrier
    join = functools.partial(jnp.concatenate, axis=1)
    moved = lax.axis_index("peer") % 2 == 1

    own = jnp.stack([tokens[0], cotangent[0]])
    own = jnp.where(moved, from_below(own), own)

    y_up, y_down = move(own, y=1), move(own, y=-1)
    along_z = own[:, :FIRST]
    z_up, z_down = move(along_z, z=1), move(along_z, z=-1)

    weights = jnp.concatenate([gate_weight[0], up_weight[0], down_weight[0]])
    own, weights = hold((own, weights))
    weights = jnp.where(moved, from_below(weights), weights)
    weights, down = weights[: 2 * ROWS], weights[2 * ROWS :]
    grads = functools.partial(add_grads, weights=weights, down=down)

    far_y = (move(y_up[:, :HALF], y=1), move(y_down[:, HALF:], y=-1))
    far_z = (move(z_up[:, :HALF], z=1), move(z_down[:, HALF:], z=-1))

    *far_y, z_up, z_down = hold((*far_y, z_up, z_down))
    near = jnp.stack([z_up, z_down])
    row = join([part[:, FIRST:] for part in (own, y_up, y_down)] + [far_y[1][:, FIRST - HALF :]])
    near, row = hold((near, row))
    near_up, near_down = move(near, y=1), move(near, y=-1)
    *far_z, row = hold((*far_z, row))
    row_up, row_down = move(row, z=1), move(row, z=-1)
    own, row = hold((own, row))
    total = grads([own, y_up, y_down, *far_y, near, *far_z])

    opposite = join(far_z)
    near_up, near_down, row_up, row_down, total = hold((near_up, near_down, row_up, row_down, total))
    last_up = move(join([near_up[0], opposite]), y=1)
    last_down = move(join([near_down[1], opposite]), y=-1)
    wide = row.shape[1] // 2
    row_far = (move(row_up[:, :wide], z=1), move(row_down[:, wide:], z=-1))
    total = grads([near_up, near_down, row_up, row_down], so_far=total)
    last_up, last_down, total = hold((last_up, last_down, total))
    opposite_far = (
        move(last_up[:, FIRST : FIRST + HALF], y=1),
        move(last_down[:, FIRST + HALF :], y=-1),
    )
    total = grads([last_up, last_down, *row_far], so_far=total)
    gate, up = grads(opposite_far, so_far=total, last=True)
    return (averaged(gate, across(gate))[None], averaged(up, across(up))[None])


def solution(mesh):
    spec = P("peer", "fsdp", None)
    return jax.shard_map(
        body,
        mesh=mesh,
        in_specs=(spec,) * 5,
        out_specs=(spec, spec),
        check_vma=False,
    )
```

```python
import functools

import jax
import jax.numpy as jnp
from jax import lax
from jax.experimental import pallas as pl
from jax.experimental.pallas import tpu as pltpu
from jax.sharding import PartitionSpec as P

D = 2048
FF = 5632
HOP = 2
ROWS = 352
FIRST = 112
HALF = 64
TILE = 256

rate_value = 1.0

AXES = ("peer", "fsdp")


def device_index(z_lo, x, core, y, z_hi):
    return ((z_lo * 4 + x) * 2 + core) * 16 + y * 4 + z_hi


def shifted(block, y=0, z=0):
    pairs = [
        (
            device_index(z_lo, x, core, at_y, at_z),
            device_index(z_lo, x, core, (at_y + y) % 4, (at_z + z) % 4),
        )
        for z_lo in range(2)
        for x in range(4)
        for core in range(2)
        for at_y in range(4)
        for at_z in range(4)
    ]
    return lax.ppermute(block, AXES, pairs)


def peer_index(z_lo, x, core):
    return (z_lo * 4 + x) * 2 + core


def from_below(block):
    pairs = [(peer_index(z_lo, x, 1), peer_index(z_lo, (x + 1) % 4, 1)) for z_lo in range(2) for x in range(4)]
    return lax.ppermute(block, "peer", pairs)


def across(block):
    peers = lax.axis_size("peer")
    pairs = [(i, (i + HOP) % peers) for i in range(0, peers, 2)]
    pairs += [(peer_index(z_lo, (x + 1) % 4, 1), peer_index(z_lo, x, 1)) for z_lo in range(2) for x in range(4)]
    return lax.ppermute(block, "peer", pairs)


def swapped(block):
    pairs = [(peer_index(z_lo, 0, 1), peer_index(1 - z_lo, 0, 1)) for z_lo in range(2)]
    return lax.ppermute(block, "peer", pairs)


def contract_last(left, right):
    return lax.dot_general(
        left, right, (((1,), (1,)), ((), ())), preferred_element_type=jnp.float32
    )


def sub_blocks(piece):
    found = [()]
    for size in piece.shape[:-3]:
        found = [index + (i,) for index in found for i in range(size)]
    return found


def add_up(count, first, last, amount, pieces, weights, down, sum_in, outs, tokens, cots, slopes, sems):
    loads = []

    def begin(source, target):
        copy = pltpu.make_async_copy(source, target, sems.at[len(loads)])
        copy.start()
        loads.append(copy)

    offset = 0
    ends = []
    for piece in pieces:
        size = piece.shape[-2]
        for index in sub_blocks(piece):
            begin(piece.at[index + (0,)], tokens.at[pl.ds(offset, size)])
            begin(piece.at[index + (1,)], cots.at[pl.ds(offset, size)])
            offset += size
            ends += [offset, offset]
    padded = tokens.shape[0]
    if padded > offset:
        tokens[offset:, :] = jnp.zeros((padded - offset, D), jnp.bfloat16)
        cots[offset:, :] = jnp.zeros((padded - offset, D), jnp.bfloat16)

    waited = 0
    for start in range(0, padded, TILE):
        size = min(TILE, padded - start)
        while waited < len(loads) and (waited == 0 or ends[waited - 1] < start + size):
            loads[waited].wait()
            loads[waited + 1].wait()
            waited += 2
        rows = pl.ds(start, size)
        both = contract_last(weights[...], tokens[rows, :]) * D ** (-0.5)
        gate, up = both[:ROWS], both[ROWS:]
        dhidden = contract_last(down[...], cots[rows, :]) * FF ** (-0.5)
        sigma = jax.nn.sigmoid(gate)
        slopes[:ROWS, rows] = (dhidden * up * sigma * (1.0 + gate * (1.0 - sigma))).astype(
            jnp.bfloat16
        )
        slopes[ROWS:, rows] = (dhidden * gate * sigma).astype(jnp.bfloat16)

    for column in range(D // TILE):
        part = pl.ds(column * TILE, TILE)
        grad = jnp.dot(slopes[...], tokens[:, part], preferred_element_type=jnp.float32)
        if not first:
            grad = sum_in[:, part] + grad
        if last:
            stepped = (
                weights[:, part].astype(jnp.float32) - rate_value * (grad * D ** (-0.5))
            ).astype(jnp.bfloat16)
            outs[0][:, part] = stepped[:ROWS]
            outs[1][:, part] = stepped[ROWS:]
        else:
            outs[0][:, part] = grad


def grad_kernel(count, first, last, amount, *refs):
    pieces = refs[:count]
    weights, down = refs[count : count + 2]
    refs = refs[count + 2 :]
    sum_in = None
    if not first:
        sum_in, refs = refs[0], refs[1:]
    wide = 2 if last else 1
    outs, scratch = refs[:wide], refs[wide:]
    add_up(count, first, last, amount, pieces, weights, down, sum_in, outs, *scratch)


def add_grads(pieces, weights, down, so_far=None, last=False):
    amount = 0
    copies = 0
    for piece in pieces:
        blocks = len(sub_blocks(piece))
        amount += blocks * piece.shape[-2]
        copies += 2 * blocks
    padded = -(-amount // 128) * 128
    first = so_far is None
    operands = list(pieces) + [weights, down] + ([] if first else [so_far])
    whole = pl.BlockSpec(memory_space=pltpu.VMEM)
    anywhere = pl.BlockSpec(memory_space=pl.ANY)
    in_specs = [anywhere] * len(pieces) + [whole] * (len(operands) - len(pieces))
    if last:
        out_shape = (jax.ShapeDtypeStruct((ROWS, D), jnp.bfloat16),) * 2
        out_specs = (whole, whole)
    else:
        out_shape = jax.ShapeDtypeStruct((2 * ROWS, D), jnp.float32)
        out_specs = whole
    return pl.pallas_call(
        functools.partial(grad_kernel, len(pieces), first, last, amount),
        out_shape=out_shape,
        in_specs=in_specs,
        out_specs=out_specs,
        input_output_aliases={} if first or last else {len(operands) - 1: 0},
        scratch_shapes=[
            pltpu.VMEM((padded, D), jnp.bfloat16),
            pltpu.VMEM((padded, D), jnp.bfloat16),
            pltpu.VMEM((2 * ROWS, padded), jnp.bfloat16),
            pltpu.SemaphoreType.DMA((copies,)),
        ],
        compiler_params=pltpu.CompilerParams(vmem_limit_bytes=24 * 1024 * 1024),
        cost_estimate=pl.CostEstimate(
            flops=10 * amount * D * ROWS, bytes_accessed=amount * D, transcendentals=0
        ),
    )(*operands)


def averaged(mine, theirs):
    return ((mine.astype(jnp.float32) + theirs.astype(jnp.float32)) * 0.5).astype(jnp.bfloat16)


def body(tokens, gate_weight, up_weight, down_weight, cotangent):
    move = shifted
    hold = lax.optimization_barrier
    join = functools.partial(jnp.concatenate, axis=1)
    place = lax.axis_index("peer")
    moved = place % 2 == 1
    at_end = place % 8 == 1

    own = jnp.stack([tokens[0], cotangent[0]])
    own = jnp.where(moved, from_below(own), own)

    y_up, y_down = move(own, y=1), move(own, y=-1)
    along_z = own[:, :FIRST]
    z_up, z_down = move(along_z, z=1), move(along_z, z=-1)

    weights = jnp.concatenate([gate_weight[0], up_weight[0], down_weight[0]])
    own, weights = hold((own, weights))
    weights = jnp.where(moved, from_below(weights), weights)
    weights, down = weights[: 2 * ROWS], weights[2 * ROWS :]
    grads = functools.partial(add_grads, weights=weights, down=down)

    far_y = (move(y_up[:, :HALF], y=1), move(y_down[:, HALF:], y=-1))
    far_z = (move(z_up[:, :HALF], z=1), move(z_down[:, HALF:], z=-1))

    *far_y, z_up, z_down = hold((*far_y, z_up, z_down))
    near = jnp.stack([z_up, z_down])
    row = join([part[:, FIRST:] for part in (own, y_up, y_down)] + [far_y[1][:, FIRST - HALF :]])
    near, row = hold((near, row))
    near_up, near_down = move(near, y=1), move(near, y=-1)
    *far_z, row = hold((*far_z, row))
    row_up, row_down = move(row, z=1), move(row, z=-1)
    own, row = hold((own, row))
    total = grads([own, y_up, y_down, *far_y, near, *far_z])

    opposite = join(far_z)
    near_up, near_down, row_up, row_down, total = hold((near_up, near_down, row_up, row_down, total))
    last_up = move(join([near_up[0], opposite]), y=1)
    last_down = move(join([near_down[1], opposite]), y=-1)
    wide = row.shape[1] // 2
    row_far = (move(row_up[:, :wide], z=1), move(row_down[:, wide:], z=-1))
    total = grads([near_up, near_down, row_up, row_down], so_far=total)
    last_up, last_down, total = hold((last_up, last_down, total))
    opposite_far = (
        move(last_up[:, FIRST : FIRST + HALF], y=1),
        move(last_down[:, FIRST + HALF :], y=-1),
    )
    total = grads([last_up, last_down, *row_far], so_far=total)
    gate, up = grads(opposite_far, so_far=total, last=True)
    got_gate, got_up = across(gate), across(up)
    gate = jnp.where(at_end, swapped(gate), gate)
    up = jnp.where(at_end, swapped(up), up)
    return (averaged(gate, got_gate)[None], averaged(up, got_up)[None])


def solution(mesh):
    spec = P("peer", "fsdp", None)
    return jax.shard_map(
        body,
        mesh=mesh,
        in_specs=(spec,) * 5,
        out_specs=(spec, spec),
        check_vma=False,
    )
```

```python
import functools

import jax
import jax.numpy as jnp
from jax import lax
from jax.experimental import pallas as pl
from jax.experimental.pallas import tpu as pltpu
from jax.sharding import PartitionSpec as P

D = 2048
FF = 5632
HOP = 2
ROWS = 352
TOKENS = 128
FIRST = 96
TILE = 256

rate_value = 1.0

AXES = ("peer", "fsdp")


def device_index(z_lo, x, core, y, z_hi):
    return ((z_lo * 4 + x) * 2 + core) * 16 + y * 4 + z_hi


def shifted(block, y=0, z=0):
    pairs = [
        (
            device_index(z_lo, x, core, at_y, at_z),
            device_index(z_lo, x, core, (at_y + y) % 4, (at_z + z) % 4),
        )
        for z_lo in range(2)
        for x in range(4)
        for core in range(2)
        for at_y in range(4)
        for at_z in range(4)
    ]
    return lax.ppermute(block, AXES, pairs)


def peer_index(z_lo, x, core):
    return (z_lo * 4 + x) * 2 + core


def from_below(block):
    pairs = [(peer_index(z_lo, x, 1), peer_index(z_lo, (x + 1) % 4, 1)) for z_lo in range(2) for x in range(4)]
    return lax.ppermute(block, "peer", pairs)


def across(block):
    peers = lax.axis_size("peer")
    pairs = [(i, (i + HOP) % peers) for i in range(0, peers, 2)]
    pairs += [(peer_index(z_lo, (x + 1) % 4, 1), peer_index(z_lo, x, 1)) for z_lo in range(2) for x in range(4)]
    return lax.ppermute(block, "peer", pairs)


def swapped(block):
    pairs = [(peer_index(z_lo, 0, 1), peer_index(1 - z_lo, 0, 1)) for z_lo in range(2)]
    return lax.ppermute(block, "peer", pairs)


def contract_last(left, right):
    return lax.dot_general(
        left, right, (((1,), (1,)), ((), ())), preferred_element_type=jnp.float32
    )


def sub_blocks(piece):
    found = [()]
    for size in piece.shape[:-3]:
        found = [index + (i,) for index in found for i in range(size)]
    return found


def add_up(count, first, last, amount, pieces, weights, down, sum_in, outs, tokens, cots, slopes, sems):
    loads = []

    def begin(source, target):
        copy = pltpu.make_async_copy(source, target, sems.at[len(loads)])
        copy.start()
        loads.append(copy)

    offset = 0
    ends = []
    for piece in pieces:
        size = piece.shape[-2]
        for index in sub_blocks(piece):
            begin(piece.at[index + (0,)], tokens.at[pl.ds(offset, size)])
            begin(piece.at[index + (1,)], cots.at[pl.ds(offset, size)])
            offset += size
            ends += [offset, offset]
    padded = tokens.shape[0]
    if padded > offset:
        tokens[offset:, :] = jnp.zeros((padded - offset, D), jnp.bfloat16)
        cots[offset:, :] = jnp.zeros((padded - offset, D), jnp.bfloat16)

    waited = 0
    for start in range(0, padded, TILE):
        size = min(TILE, padded - start)
        while waited < len(loads) and (waited == 0 or ends[waited - 1] < start + size):
            loads[waited].wait()
            loads[waited + 1].wait()
            waited += 2
        rows = pl.ds(start, size)
        both = contract_last(weights[...], tokens[rows, :]) * D ** (-0.5)
        gate, up = both[:ROWS], both[ROWS:]
        dhidden = contract_last(down[...], cots[rows, :]) * FF ** (-0.5)
        sigma = jax.nn.sigmoid(gate)
        slopes[:ROWS, rows] = (dhidden * up * sigma * (1.0 + gate * (1.0 - sigma))).astype(
            jnp.bfloat16
        )
        slopes[ROWS:, rows] = (dhidden * gate * sigma).astype(jnp.bfloat16)

    for column in range(D // TILE):
        part = pl.ds(column * TILE, TILE)
        grad = jnp.dot(slopes[...], tokens[:, part], preferred_element_type=jnp.float32)
        if not first:
            grad = sum_in[:, part] + grad
        if last:
            stepped = (
                weights[:, part].astype(jnp.float32) - rate_value * (grad * D ** (-0.5))
            ).astype(jnp.bfloat16)
            outs[0][:, part] = stepped[:ROWS]
            outs[1][:, part] = stepped[ROWS:]
        else:
            outs[0][:, part] = grad


def grad_kernel(count, first, last, amount, *refs):
    pieces = refs[:count]
    weights, down = refs[count : count + 2]
    refs = refs[count + 2 :]
    sum_in = None
    if not first:
        sum_in, refs = refs[0], refs[1:]
    wide = 2 if last else 1
    outs, scratch = refs[:wide], refs[wide:]
    add_up(count, first, last, amount, pieces, weights, down, sum_in, outs, *scratch)


def add_grads(pieces, weights, down, so_far=None, last=False):
    amount = 0
    copies = 0
    for piece in pieces:
        blocks = len(sub_blocks(piece))
        amount += blocks * piece.shape[-2]
        copies += 2 * blocks
    padded = -(-amount // 128) * 128
    first = so_far is None
    operands = list(pieces) + [weights, down] + ([] if first else [so_far])
    whole = pl.BlockSpec(memory_space=pltpu.VMEM)
    anywhere = pl.BlockSpec(memory_space=pl.ANY)
    in_specs = [anywhere] * len(pieces) + [whole] * (len(operands) - len(pieces))
    if last:
        out_shape = (jax.ShapeDtypeStruct((ROWS, D), jnp.bfloat16),) * 2
        out_specs = (whole, whole)
    else:
        out_shape = jax.ShapeDtypeStruct((2 * ROWS, D), jnp.float32)
        out_specs = whole
    return pl.pallas_call(
        functools.partial(grad_kernel, len(pieces), first, last, amount),
        out_shape=out_shape,
        in_specs=in_specs,
        out_specs=out_specs,
        input_output_aliases={} if first or last else {len(operands) - 1: 0},
        scratch_shapes=[
            pltpu.VMEM((padded, D), jnp.bfloat16),
            pltpu.VMEM((padded, D), jnp.bfloat16),
            pltpu.VMEM((2 * ROWS, padded), jnp.bfloat16),
            pltpu.SemaphoreType.DMA((copies,)),
        ],
        compiler_params=pltpu.CompilerParams(vmem_limit_bytes=24 * 1024 * 1024),
        cost_estimate=pl.CostEstimate(
            flops=10 * amount * D * ROWS, bytes_accessed=amount * D, transcendentals=0
        ),
    )(*operands)


def averaged(mine, theirs):
    return ((mine.astype(jnp.float32) + theirs.astype(jnp.float32)) * 0.5).astype(jnp.bfloat16)


def body(tokens, gate_weight, up_weight, down_weight, cotangent):
    move = shifted
    hold = lax.optimization_barrier
    join = functools.partial(jnp.concatenate, axis=1)
    place = lax.axis_index("peer")
    moved = place % 2 == 1
    at_end = place % 8 == 1

    pair = (tokens[0], cotangent[0])
    below = from_below(pair)
    own = jnp.stack([jnp.where(moved, theirs, mine) for theirs, mine in zip(below, pair)])

    weights = jnp.concatenate([gate_weight[0], up_weight[0], down_weight[0]])
    own, weights = hold((own, weights))
    weights = jnp.where(moved, from_below(weights), weights)
    weights, down = weights[: 2 * ROWS], weights[2 * ROWS :]
    grads = functools.partial(add_grads, weights=weights, down=down)

    y_up, y_down = move(own, y=1), move(own, y=-1)
    along_z = own[:, :FIRST]
    z_up, z_down = move(along_z, z=1), move(along_z, z=-1)

    half = TOKENS // 2
    far_y = (move(y_up[:, :half], y=1), move(y_down[:, half:], y=-1))
    half = FIRST // 2
    far_z = (move(z_up[:, :half], z=1), move(z_down[:, half:], z=-1))
    *far_y, z_up, z_down = hold((*far_y, z_up, z_down))
    near = jnp.stack([z_up, z_down])
    row = [part[:, FIRST:] for part in (own, y_up, y_down)] + [far_y[1][:, FIRST - TOKENS // 2 :]]
    row, rest = join(row[:2]), join(row[2:])
    near, row, rest = hold((near, row, rest))
    near_up, near_down = move(near, y=1), move(near, y=-1)
    *far_z, row = hold((*far_z, row))
    row_up, row_down = move(row, z=1), move(row, z=-1)
    own, row = hold((own, row))
    total = grads([own, y_up, y_down, *far_y, near, *far_z])

    opposite = join(far_z)
    near_up, near_down, row_up, row_down, rest, total = hold((near_up, near_down, row_up, row_down, rest, total))
    last_up = move(join([near_up[0], opposite]), y=1)
    last_down = move(join([near_down[1], opposite]), y=-1)
    rest_up, rest_down = move(rest, z=1), move(rest, z=-1)
    total = grads([near_up, near_down, row_up, row_down], so_far=total)
    last_up, last_down, rest_up, rest_down, total = hold((last_up, last_down, rest_up, rest_down, total))
    opposite_far = (
        move(last_up[:, FIRST : FIRST + half], y=1),
        move(last_down[:, FIRST + half :], y=-1),
    )
    row_far = (move(row_up, z=1), move(rest_down, z=-1))
    total = grads([last_up, last_down, rest_up, rest_down], so_far=total)
    gate, up = grads([*opposite_far, *row_far], so_far=total, last=True)
    got_gate, got_up = across(gate), across(up)
    gate = jnp.where(at_end, swapped(gate), gate)
    up = jnp.where(at_end, swapped(up), up)
    return (averaged(gate, got_gate)[None], averaged(up, got_up)[None])


def solution(mesh):
    spec = P("peer", "fsdp", None)
    return jax.shard_map(
        body,
        mesh=mesh,
        in_specs=(spec,) * 5,
        out_specs=(spec, spec),
        check_vma=False,
    )
```

```python
import functools

import jax
import jax.numpy as jnp
from jax import lax
from jax.experimental import pallas as pl
from jax.experimental.pallas import tpu as pltpu
from jax.sharding import PartitionSpec as P

D = 2048
FF = 5632
HOP = 2
ROWS = 352
TOKENS = 128
FIRST = 96
TILE = 256

rate_value = 1.0

AXES = ("peer", "fsdp")


def device_index(z_lo, x, core, y, z_hi):
    return ((z_lo * 4 + x) * 2 + core) * 16 + y * 4 + z_hi


def shifted(block, y=0, z=0):
    pairs = [
        (
            device_index(z_lo, x, core, at_y, at_z),
            device_index(z_lo, x, core, (at_y + y) % 4, (at_z + z) % 4),
        )
        for z_lo in range(2)
        for x in range(4)
        for core in range(2)
        for at_y in range(4)
        for at_z in range(4)
    ]
    return lax.ppermute(block, AXES, pairs)


def peer_index(z_lo, x, core):
    return (z_lo * 4 + x) * 2 + core


def from_below(block):
    pairs = [(peer_index(z_lo, x, 1), peer_index(z_lo, (x + 1) % 4, 1)) for z_lo in range(2) for x in range(4)]
    return lax.ppermute(block, "peer", pairs)


def across(block):
    peers = lax.axis_size("peer")
    pairs = [(i, (i + HOP) % peers) for i in range(0, peers, 2)]
    pairs += [(peer_index(z_lo, (x + 1) % 4, 1), peer_index(z_lo, x, 1)) for z_lo in range(2) for x in range(4)]
    return lax.ppermute(block, "peer", pairs)


def swapped(block):
    pairs = [(peer_index(z_lo, 0, 1), peer_index(1 - z_lo, 0, 1)) for z_lo in range(2)]
    return lax.ppermute(block, "peer", pairs)


def contract_last(left, right):
    return lax.dot_general(
        left, right, (((1,), (1,)), ((), ())), preferred_element_type=jnp.float32
    )


def sub_blocks(piece):
    found = [()]
    for size in piece.shape[:-3]:
        found = [index + (i,) for index in found for i in range(size)]
    return found


def add_up(count, first, last, amount, pieces, weights, down, sum_in, outs, tokens, cots, slopes, sems):
    loads = []

    def begin(source, target):
        copy = pltpu.make_async_copy(source, target, sems.at[len(loads)])
        copy.start()
        loads.append(copy)

    offset = 0
    ends = []
    for piece in pieces:
        size = piece.shape[-2]
        for index in sub_blocks(piece):
            begin(piece.at[index + (0,)], tokens.at[pl.ds(offset, size)])
            begin(piece.at[index + (1,)], cots.at[pl.ds(offset, size)])
            offset += size
            ends += [offset, offset]
    padded = tokens.shape[0]
    if padded > offset:
        tokens[offset:, :] = jnp.zeros((padded - offset, D), jnp.bfloat16)
        cots[offset:, :] = jnp.zeros((padded - offset, D), jnp.bfloat16)

    waited = 0
    for start in range(0, padded, TILE):
        size = min(TILE, padded - start)
        while waited < len(loads) and (waited == 0 or ends[waited - 1] < start + size):
            loads[waited].wait()
            loads[waited + 1].wait()
            waited += 2
        rows = pl.ds(start, size)
        both = contract_last(weights[...], tokens[rows, :]) * D ** (-0.5)
        gate, up = both[:ROWS], both[ROWS:]
        dhidden = contract_last(down[...], cots[rows, :]) * FF ** (-0.5)
        sigma = jax.nn.sigmoid(gate)
        slopes[:ROWS, rows] = (dhidden * up * sigma * (1.0 + gate * (1.0 - sigma))).astype(
            jnp.bfloat16
        )
        slopes[ROWS:, rows] = (dhidden * gate * sigma).astype(jnp.bfloat16)

    for column in range(D // TILE):
        part = pl.ds(column * TILE, TILE)
        grad = jnp.dot(slopes[...], tokens[:, part], preferred_element_type=jnp.float32)
        if not first:
            grad = sum_in[:, part] + grad
        if last:
            stepped = (
                weights[:, part].astype(jnp.float32) - rate_value * (grad * D ** (-0.5))
            ).astype(jnp.bfloat16)
            outs[0][:, part] = stepped[:ROWS]
            outs[1][:, part] = stepped[ROWS:]
        else:
            outs[0][:, part] = grad


def grad_kernel(count, first, last, amount, *refs):
    pieces = refs[:count]
    weights, down = refs[count : count + 2]
    refs = refs[count + 2 :]
    sum_in = None
    if not first:
        sum_in, refs = refs[0], refs[1:]
    wide = 2 if last else 1
    outs, scratch = refs[:wide], refs[wide:]
    add_up(count, first, last, amount, pieces, weights, down, sum_in, outs, *scratch)


def add_grads(pieces, weights, down, so_far=None, last=False):
    amount = 0
    copies = 0
    for piece in pieces:
        blocks = len(sub_blocks(piece))
        amount += blocks * piece.shape[-2]
        copies += 2 * blocks
    padded = -(-amount // 128) * 128
    first = so_far is None
    operands = list(pieces) + [weights, down] + ([] if first else [so_far])
    whole = pl.BlockSpec(memory_space=pltpu.VMEM)
    anywhere = pl.BlockSpec(memory_space=pl.ANY)
    in_specs = [anywhere] * len(pieces) + [whole] * (len(operands) - len(pieces))
    if last:
        out_shape = (jax.ShapeDtypeStruct((ROWS, D), jnp.bfloat16),) * 2
        out_specs = (whole, whole)
    else:
        out_shape = jax.ShapeDtypeStruct((2 * ROWS, D), jnp.float32)
        out_specs = whole
    return pl.pallas_call(
        functools.partial(grad_kernel, len(pieces), first, last, amount),
        out_shape=out_shape,
        in_specs=in_specs,
        out_specs=out_specs,
        input_output_aliases={} if first or last else {len(operands) - 1: 0},
        scratch_shapes=[
            pltpu.VMEM((padded, D), jnp.bfloat16),
            pltpu.VMEM((padded, D), jnp.bfloat16),
            pltpu.VMEM((2 * ROWS, padded), jnp.bfloat16),
            pltpu.SemaphoreType.DMA((copies,)),
        ],
        compiler_params=pltpu.CompilerParams(vmem_limit_bytes=24 * 1024 * 1024),
        cost_estimate=pl.CostEstimate(
            flops=10 * amount * D * ROWS, bytes_accessed=amount * D, transcendentals=0
        ),
    )(*operands)


def averaged(mine, theirs):
    return ((mine.astype(jnp.float32) + theirs.astype(jnp.float32)) * 0.5).astype(jnp.bfloat16)


def body(tokens, gate_weight, up_weight, down_weight, cotangent):
    move = shifted
    hold = lax.optimization_barrier
    join = functools.partial(jnp.concatenate, axis=1)
    place = lax.axis_index("peer")
    moved = place % 2 == 1
    at_end = place % 8 == 1

    own = jnp.stack([tokens[0], cotangent[0]])
    own = jnp.where(moved, from_below(own), own)

    y_up, y_down = move(own, y=1), move(own, y=-1)
    along_z = own[:, :FIRST]
    z_up, z_down = move(along_z, z=1), move(along_z, z=-1)

    half = TOKENS // 2
    y_up, y_down, *weights = hold((y_up, y_down, gate_weight[0], up_weight[0], down_weight[0]))
    far_y = (move(y_up[:, :half], y=1), move(y_down[:, half:], y=-1))
    weights = jnp.concatenate(weights)

    half = FIRST // 2
    far_z = (move(z_up[:, :half], z=1), move(z_down[:, half:], z=-1))
    *far_y, z_up, z_down, weights = hold((*far_y, z_up, z_down, weights))
    near = jnp.stack([z_up, z_down])
    row = [part[:, FIRST:] for part in (own, y_up, y_down)] + [far_y[1][:, FIRST - TOKENS // 2 :]]
    row, rest = join(row[:2]), join(row[2:])
    near_up, near_down = move(near, y=1), move(near, y=-1)
    weights = jnp.where(moved, from_below(weights), weights)
    weights, down = weights[: 2 * ROWS], weights[2 * ROWS :]
    grads = functools.partial(add_grads, weights=weights, down=down)
    *far_z, row = hold((*far_z, row))
    row_up, row_down = move(row, z=1), move(row, z=-1)

    opposite = join(far_z)
    near_up, near_down, row_up, row_down, rest = hold((near_up, near_down, row_up, row_down, rest))
    last_up = move(join([near_up[0], opposite]), y=1)
    last_down = move(join([near_down[1], opposite]), y=-1)
    wide = row.shape[1] // 2
    rest_up = move(join([rest, row_up[:, :wide]]), z=1)
    rest_down = move(join([rest, row_down[:, wide:]]), z=-1)
    total = grads([own, y_up, y_down, *far_y, near, *far_z])
    total = grads([near_up, near_down, row_up, row_down], so_far=total)
    last_up, last_down, rest_up, rest_down, total = hold((last_up, last_down, rest_up, rest_down, total))
    opposite_far = (
        move(last_up[:, FIRST : FIRST + half], y=1),
        move(last_down[:, FIRST + half :], y=-1),
    )
    rest_far = (move(rest_up[:, :wide], z=1), move(rest_down[:, wide : 2 * wide], z=-1))
    total = grads([last_up, last_down, rest_up, rest_down], so_far=total)
    gate, up = grads([*opposite_far, *rest_far], so_far=total, last=True)
    got_gate, got_up = across(gate), across(up)
    gate = jnp.where(at_end, swapped(gate), gate)
    up = jnp.where(at_end, swapped(up), up)
    return (averaged(gate, got_gate)[None], averaged(up, got_up)[None])


def solution(mesh):
    spec = P("peer", "fsdp", None)
    return jax.shard_map(
        body,
        mesh=mesh,
        in_specs=(spec,) * 5,
        out_specs=(spec, spec),
        check_vma=False,
    )
```

```python
import functools

import jax
import jax.numpy as jnp
from jax import lax
from jax.experimental import pallas as pl
from jax.experimental.pallas import tpu as pltpu
from jax.sharding import PartitionSpec as P

D = 2048
FF = 5632
HOP = 2
ROWS = 352
TOKENS = 128
FIRST = 96
TILE = 256

rate_value = 1.0

AXES = ("peer", "fsdp")


def device_index(z_lo, x, core, y, z_hi):
    return ((z_lo * 4 + x) * 2 + core) * 16 + y * 4 + z_hi


def shifted(block, y=0, z=0):
    pairs = [
        (
            device_index(z_lo, x, core, at_y, at_z),
            device_index(z_lo, x, core, (at_y + y) % 4, (at_z + z) % 4),
        )
        for z_lo in range(2)
        for x in range(4)
        for core in range(2)
        for at_y in range(4)
        for at_z in range(4)
    ]
    return lax.ppermute(block, AXES, pairs)


def peer_index(z_lo, x, core):
    return (z_lo * 4 + x) * 2 + core


def from_below(block):
    pairs = [(peer_index(z_lo, x, 1), peer_index(z_lo, (x + 1) % 4, 1)) for z_lo in range(2) for x in range(4)]
    return lax.ppermute(block, "peer", pairs)


def from_other_core(block):
    peers = lax.axis_size("peer")
    return lax.ppermute(block, "peer", [(i + 1, i) for i in range(0, peers, 2)])


def across(block):
    peers = lax.axis_size("peer")
    pairs = [(i, (i + HOP) % peers) for i in range(0, peers, 2)]
    pairs += [(peer_index(z_lo, (x + 1) % 4, 1), peer_index(z_lo, x, 1)) for z_lo in range(2) for x in range(4)]
    return lax.ppermute(block, "peer", pairs)


def swapped(block):
    pairs = [(peer_index(z_lo, 0, 1), peer_index(1 - z_lo, 0, 1)) for z_lo in range(2)]
    return lax.ppermute(block, "peer", pairs)


def contract_last(left, right):
    return lax.dot_general(
        left, right, (((1,), (1,)), ((), ())), preferred_element_type=jnp.float32
    )


def sub_blocks(piece):
    found = [()]
    for size in piece.shape[:-3]:
        found = [index + (i,) for index in found for i in range(size)]
    return found


def add_up(count, first, last, amount, pieces, weights, down, sum_in, outs, tokens, cots, slopes, sems):
    loads = []

    def begin(source, target):
        copy = pltpu.make_async_copy(source, target, sems.at[len(loads)])
        copy.start()
        loads.append(copy)

    offset = 0
    ends = []
    for piece in pieces:
        size = piece.shape[-2]
        for index in sub_blocks(piece):
            begin(piece.at[index + (0,)], tokens.at[pl.ds(offset, size)])
            begin(piece.at[index + (1,)], cots.at[pl.ds(offset, size)])
            offset += size
            ends += [offset, offset]
    padded = tokens.shape[0]
    if padded > offset:
        tokens[offset:, :] = jnp.zeros((padded - offset, D), jnp.bfloat16)
        cots[offset:, :] = jnp.zeros((padded - offset, D), jnp.bfloat16)

    waited = 0
    for start in range(0, padded, TILE):
        size = min(TILE, padded - start)
        while waited < len(loads) and (waited == 0 or ends[waited - 1] < start + size):
            loads[waited].wait()
            loads[waited + 1].wait()
            waited += 2
        rows = pl.ds(start, size)
        both = contract_last(weights[...], tokens[rows, :]) * D ** (-0.5)
        gate, up = both[:ROWS], both[ROWS:]
        dhidden = contract_last(down[...], cots[rows, :]) * FF ** (-0.5)
        sigma = jax.nn.sigmoid(gate)
        slopes[:ROWS, rows] = (dhidden * up * sigma * (1.0 + gate * (1.0 - sigma))).astype(
            jnp.bfloat16
        )
        slopes[ROWS:, rows] = (dhidden * gate * sigma).astype(jnp.bfloat16)

    for column in range(D // TILE):
        part = pl.ds(column * TILE, TILE)
        grad = jnp.dot(slopes[...], tokens[:, part], preferred_element_type=jnp.float32)
        if not first:
            grad = sum_in[:, part] + grad
        if last:
            stepped = (
                weights[:, part].astype(jnp.float32) - rate_value * (grad * D ** (-0.5))
            ).astype(jnp.bfloat16)
            outs[0][:, part] = stepped[:ROWS]
            outs[1][:, part] = stepped[ROWS:]
        else:
            outs[0][:, part] = grad


def grad_kernel(count, first, last, amount, *refs):
    pieces = refs[:count]
    weights, down = refs[count : count + 2]
    refs = refs[count + 2 :]
    sum_in = None
    if not first:
        sum_in, refs = refs[0], refs[1:]
    wide = 2 if last else 1
    outs, scratch = refs[:wide], refs[wide:]
    add_up(count, first, last, amount, pieces, weights, down, sum_in, outs, *scratch)


def add_grads(pieces, weights, down, so_far=None, last=False):
    amount = 0
    copies = 0
    for piece in pieces:
        blocks = len(sub_blocks(piece))
        amount += blocks * piece.shape[-2]
        copies += 2 * blocks
    padded = -(-amount // 128) * 128
    first = so_far is None
    operands = list(pieces) + [weights, down] + ([] if first else [so_far])
    whole = pl.BlockSpec(memory_space=pltpu.VMEM)
    anywhere = pl.BlockSpec(memory_space=pl.ANY)
    in_specs = [anywhere] * len(pieces) + [whole] * (len(operands) - len(pieces))
    if last:
        out_shape = (jax.ShapeDtypeStruct((ROWS, D), jnp.bfloat16),) * 2
        out_specs = (whole, whole)
    else:
        out_shape = jax.ShapeDtypeStruct((2 * ROWS, D), jnp.float32)
        out_specs = whole
    return pl.pallas_call(
        functools.partial(grad_kernel, len(pieces), first, last, amount),
        out_shape=out_shape,
        in_specs=in_specs,
        out_specs=out_specs,
        input_output_aliases={} if first or last else {len(operands) - 1: 0},
        scratch_shapes=[
            pltpu.VMEM((padded, D), jnp.bfloat16),
            pltpu.VMEM((padded, D), jnp.bfloat16),
            pltpu.VMEM((2 * ROWS, padded), jnp.bfloat16),
            pltpu.SemaphoreType.DMA((copies,)),
        ],
        compiler_params=pltpu.CompilerParams(vmem_limit_bytes=24 * 1024 * 1024),
        cost_estimate=pl.CostEstimate(
            flops=10 * amount * D * ROWS, bytes_accessed=amount * D, transcendentals=0
        ),
    )(*operands)


def averaged(mine, theirs):
    return ((mine.astype(jnp.float32) + theirs.astype(jnp.float32)) * 0.5).astype(jnp.bfloat16)


def body(tokens, gate_weight, up_weight, down_weight, cotangent):
    move = shifted
    hold = lax.optimization_barrier
    join = functools.partial(jnp.concatenate, axis=1)
    place = lax.axis_index("peer")
    moved = place % 2 == 1

    own = jnp.stack([tokens[0], cotangent[0]])
    own = jnp.where(moved, from_below(own), own)

    y_up, y_down = move(own, y=1), move(own, y=-1)
    along_z = own[:, :FIRST]
    z_up, z_down = move(along_z, z=1), move(along_z, z=-1)

    half = TOKENS // 2
    y_up, y_down, *weights = hold((y_up, y_down, gate_weight[0], up_weight[0], down_weight[0]))
    far_y = (move(y_up[:, :half], y=1), move(y_down[:, half:], y=-1))
    weights = jnp.concatenate(weights)

    half = FIRST // 2
    far_z = (move(z_up[:, :half], z=1), move(z_down[:, half:], z=-1))
    *far_y, z_up, z_down, weights = hold((*far_y, z_up, z_down, weights))
    near = jnp.stack([z_up, z_down])
    near, told = hold((near, from_other_core(near[0, 0, :16])))
    row = [part[:, FIRST:] for part in (own, y_up, y_down)] + [far_y[1][:, FIRST - TOKENS // 2 :]]
    row, rest = join(row[:2]), join(row[2:])
    near_up, near_down = move(near, y=1), move(near, y=-1)
    weights = jnp.where(moved, from_below(weights), weights)
    weights, down = weights[: 2 * ROWS], weights[2 * ROWS :]
    grads = functools.partial(add_grads, weights=weights, down=down)
    *far_z, row = hold((*far_z, row))
    row_up, row_down = move(row, z=1), move(row, z=-1)

    opposite = join(far_z)
    near_up, near_down, row_up, row_down, rest = hold((near_up, near_down, row_up, row_down, rest))
    last_up = move(join([near_up[0], opposite]), y=1)
    last_down = move(join([near_down[1], opposite]), y=-1)
    wide = row.shape[1] // 2
    rest_up = move(join([rest, row_up[:, :wide]]), z=1)
    rest_down = move(join([rest, row_down[:, wide:]]), z=-1)
    total = grads([own, y_up, y_down, *far_y, near, *far_z])
    total = grads([near_up, near_down, row_up, row_down], so_far=total)
    last_up, last_down, rest_up, rest_down, total = hold((last_up, last_down, rest_up, rest_down, total))
    opposite_far = (
        move(last_up[:, FIRST : FIRST + half], y=1),
        move(last_down[:, FIRST + half :], y=-1),
    )
    rest_far = (move(rest_up[:, :wide], z=1), move(rest_down[:, wide : 2 * wide], z=-1))
    total = grads([last_up, last_down, rest_up, rest_down], so_far=total)
    gate, up = grads([*opposite_far, *rest_far], so_far=total, last=True)
    got_gate, got_up = across(gate), across(up)
    at_end = (place % 8 == 1) & (told[0, 0] < 128.0)
    gate = jnp.where(at_end, swapped(gate), gate)
    up = jnp.where(at_end, swapped(up), up)
    return (averaged(gate, got_gate)[None], averaged(up, got_up)[None])


def solution(mesh):
    spec = P("peer", "fsdp", None)
    return jax.shard_map(
        body,
        mesh=mesh,
        in_specs=(spec,) * 5,
        out_specs=(spec, spec),
        check_vma=False,
    )
```

```python
import functools

import jax
import jax.numpy as jnp
from jax import lax
from jax.experimental import pallas as pl
from jax.experimental.pallas import tpu as pltpu
from jax.sharding import PartitionSpec as P

D = 2048
FF = 5632
HOP = 2
ROWS = 352
TOKENS = 128
FIRST = 96
TILE = 256

rate_value = 1.0

AXES = ("peer", "fsdp")


def device_index(z_lo, x, core, y, z_hi):
    return ((z_lo * 4 + x) * 2 + core) * 16 + y * 4 + z_hi


def shifted(block, y=0, z=0):
    pairs = [
        (
            device_index(z_lo, x, core, at_y, at_z),
            device_index(z_lo, x, core, (at_y + y) % 4, (at_z + z) % 4),
        )
        for z_lo in range(2)
        for x in range(4)
        for core in range(2)
        for at_y in range(4)
        for at_z in range(4)
    ]
    return lax.ppermute(block, AXES, pairs)


def peer_index(z_lo, x, core):
    return (z_lo * 4 + x) * 2 + core


def from_below(block):
    pairs = [(peer_index(z_lo, x, 1), peer_index(z_lo, (x + 1) % 4, 1)) for z_lo in range(2) for x in range(4)]
    return lax.ppermute(block, "peer", pairs)


def from_other_core(block):
    peers = lax.axis_size("peer")
    return lax.ppermute(block, "peer", [(i + 1, i) for i in range(0, peers, 2)])


def across(block):
    peers = lax.axis_size("peer")
    pairs = [(i, (i + HOP) % peers) for i in range(0, peers, 2)]
    pairs += [(peer_index(z_lo, (x + 1) % 4, 1), peer_index(z_lo, x, 1)) for z_lo in range(2) for x in range(4)]
    return lax.ppermute(block, "peer", pairs)


def swapped(block):
    pairs = [(peer_index(z_lo, 0, 1), peer_index(1 - z_lo, 0, 1)) for z_lo in range(2)]
    return lax.ppermute(block, "peer", pairs)


def contract_last(left, right):
    return lax.dot_general(
        left, right, (((1,), (1,)), ((), ())), preferred_element_type=jnp.float32
    )


def sub_blocks(piece):
    found = [()]
    for size in piece.shape[:-3]:
        found = [index + (i,) for index in found for i in range(size)]
    return found


def add_up(count, first, last, amount, pieces, weights, down, sum_in, outs, tokens, cots, slopes, sems):
    loads = []

    def begin(source, target):
        copy = pltpu.make_async_copy(source, target, sems.at[len(loads)])
        copy.start()
        loads.append(copy)

    offset = 0
    ends = []
    for piece in pieces:
        size = piece.shape[-2]
        for index in sub_blocks(piece):
            begin(piece.at[index + (0,)], tokens.at[pl.ds(offset, size)])
            begin(piece.at[index + (1,)], cots.at[pl.ds(offset, size)])
            offset += size
            ends += [offset, offset]
    padded = tokens.shape[0]
    if padded > offset:
        tokens[offset:, :] = jnp.zeros((padded - offset, D), jnp.bfloat16)
        cots[offset:, :] = jnp.zeros((padded - offset, D), jnp.bfloat16)

    waited = 0
    for start in range(0, padded, TILE):
        size = min(TILE, padded - start)
        while waited < len(loads) and (waited == 0 or ends[waited - 1] < start + size):
            loads[waited].wait()
            loads[waited + 1].wait()
            waited += 2
        rows = pl.ds(start, size)
        both = contract_last(weights[...], tokens[rows, :]) * D ** (-0.5)
        gate, up = both[:ROWS], both[ROWS:]
        dhidden = contract_last(down[...], cots[rows, :]) * FF ** (-0.5)
        sigma = jax.nn.sigmoid(gate)
        slopes[:ROWS, rows] = (dhidden * up * sigma * (1.0 + gate * (1.0 - sigma))).astype(
            jnp.bfloat16
        )
        slopes[ROWS:, rows] = (dhidden * gate * sigma).astype(jnp.bfloat16)

    for column in range(D // TILE):
        part = pl.ds(column * TILE, TILE)
        grad = jnp.dot(slopes[...], tokens[:, part], preferred_element_type=jnp.float32)
        if not first:
            grad = sum_in[:, part] + grad
        if last:
            stepped = (
                weights[:, part].astype(jnp.float32) - rate_value * (grad * D ** (-0.5))
            ).astype(jnp.bfloat16)
            outs[0][:, part] = stepped[:ROWS]
            outs[1][:, part] = stepped[ROWS:]
        else:
            outs[0][:, part] = grad


def grad_kernel(count, first, last, amount, *refs):
    pieces = refs[:count]
    weights, down = refs[count : count + 2]
    refs = refs[count + 2 :]
    sum_in = None
    if not first:
        sum_in, refs = refs[0], refs[1:]
    wide = 2 if last else 1
    outs, scratch = refs[:wide], refs[wide:]
    add_up(count, first, last, amount, pieces, weights, down, sum_in, outs, *scratch)


def add_grads(pieces, weights, down, so_far=None, last=False):
    amount = 0
    copies = 0
    for piece in pieces:
        blocks = len(sub_blocks(piece))
        amount += blocks * piece.shape[-2]
        copies += 2 * blocks
    padded = -(-amount // 128) * 128
    first = so_far is None
    operands = list(pieces) + [weights, down] + ([] if first else [so_far])
    whole = pl.BlockSpec(memory_space=pltpu.VMEM)
    anywhere = pl.BlockSpec(memory_space=pl.ANY)
    in_specs = [anywhere] * len(pieces) + [whole] * (len(operands) - len(pieces))
    if last:
        out_shape = (jax.ShapeDtypeStruct((ROWS, D), jnp.bfloat16),) * 2
        out_specs = (whole, whole)
    else:
        out_shape = jax.ShapeDtypeStruct((2 * ROWS, D), jnp.float32)
        out_specs = whole
    return pl.pallas_call(
        functools.partial(grad_kernel, len(pieces), first, last, amount),
        out_shape=out_shape,
        in_specs=in_specs,
        out_specs=out_specs,
        input_output_aliases={} if first or last else {len(operands) - 1: 0},
        scratch_shapes=[
            pltpu.VMEM((padded, D), jnp.bfloat16),
            pltpu.VMEM((padded, D), jnp.bfloat16),
            pltpu.VMEM((2 * ROWS, padded), jnp.bfloat16),
            pltpu.SemaphoreType.DMA((copies,)),
        ],
        compiler_params=pltpu.CompilerParams(vmem_limit_bytes=24 * 1024 * 1024),
        cost_estimate=pl.CostEstimate(
            flops=10 * amount * D * ROWS, bytes_accessed=amount * D, transcendentals=0
        ),
    )(*operands)


def averaged(mine, theirs):
    return ((mine.astype(jnp.float32) + theirs.astype(jnp.float32)) * 0.5).astype(jnp.bfloat16)


def body(tokens, gate_weight, up_weight, down_weight, cotangent):
    move = shifted
    hold = lax.optimization_barrier
    join = functools.partial(jnp.concatenate, axis=1)
    place = lax.axis_index("peer")
    moved = place % 2 == 1

    own = jnp.stack([tokens[0], cotangent[0]])
    own = jnp.where(moved, from_below(own), own)

    weights = jnp.concatenate([gate_weight[0], up_weight[0], down_weight[0]])
    own, weights = hold((own, weights))
    weights = jnp.where(moved, from_below(weights), weights)
    weights, down = weights[: 2 * ROWS], weights[2 * ROWS :]
    grads = functools.partial(add_grads, weights=weights, down=down)

    y_up, y_down = move(own, y=1), move(own, y=-1)
    along_z = own[:, :FIRST]
    z_up, z_down = move(along_z, z=1), move(along_z, z=-1)

    half = TOKENS // 2
    far_y = (move(y_up[:, :half], y=1), move(y_down[:, half:], y=-1))
    half = FIRST // 2
    far_z = (move(z_up[:, :half], z=1), move(z_down[:, half:], z=-1))
    *far_y, z_up, z_down = hold((*far_y, z_up, z_down))
    near = jnp.stack([z_up, z_down])
    row = [part[:, FIRST:] for part in (own, y_up, y_down)] + [far_y[1][:, FIRST - TOKENS // 2 :]]
    row, rest = join(row[:2]), join(row[2:])
    near, row, rest, told = hold((near, row, rest, from_other_core(near[0, 0, :16])))
    near_up, near_down = move(near, y=1), move(near, y=-1)
    *far_z, row = hold((*far_z, row))
    row_up, row_down = move(row, z=1), move(row, z=-1)
    own, row = hold((own, row))
    total = grads([own, y_up, y_down, *far_y, near, *far_z])

    opposite = join(far_z)
    near_up, near_down, row_up, row_down, rest, total = hold((near_up, near_down, row_up, row_down, rest, total))
    last_up = move(join([near_up[0], opposite]), y=1)
    last_down = move(join([near_down[1], opposite]), y=-1)
    wide = row.shape[1] // 2
    rest_up = move(join([rest, row_up[:, :wide]]), z=1)
    rest_down = move(join([rest, row_down[:, wide:]]), z=-1)
    total = grads([near_up, near_down, row_up, row_down], so_far=total)
    last_up, last_down, rest_up, rest_down, total = hold((last_up, last_down, rest_up, rest_down, total))
    opposite_far = (
        move(last_up[:, FIRST : FIRST + half], y=1),
        move(last_down[:, FIRST + half :], y=-1),
    )
    row_far = (move(rest_up[:, :wide], z=1), move(rest_down[:, wide : 2 * wide], z=-1))
    total = grads([last_up, last_down, rest_up, rest_down], so_far=total)
    gate, up = grads([*opposite_far, *row_far], so_far=total, last=True)
    got_gate, got_up = across(gate), across(up)
    at_end = (place % 8 == 1) & (told[0, 0] < 128.0)
    gate = jnp.where(at_end, swapped(gate), gate)
    up = jnp.where(at_end, swapped(up), up)
    return (averaged(gate, got_gate)[None], averaged(up, got_up)[None])


def solution(mesh):
    spec = P("peer", "fsdp", None)
    return jax.shard_map(
        body,
        mesh=mesh,
        in_specs=(spec,) * 5,
        out_specs=(spec, spec),
        check_vma=False,
    )
```

```python
import functools

import jax
import jax.numpy as jnp
from jax import lax
from jax.experimental import pallas as pl
from jax.experimental.pallas import tpu as pltpu
from jax.sharding import PartitionSpec as P

D = 2048
FF = 5632
HOP = 2
ROWS = 352
TOKENS = 128
FIRST = 96
TILE = 256

rate_value = 1.0

AXES = ("peer", "fsdp")


def device_index(z_lo, x, core, y, z_hi):
    return ((z_lo * 4 + x) * 2 + core) * 16 + y * 4 + z_hi


def shifted(block, y=0, z=0):
    pairs = [
        (
            device_index(z_lo, x, core, at_y, at_z),
            device_index(z_lo, x, core, (at_y + y) % 4, (at_z + z) % 4),
        )
        for z_lo in range(2)
        for x in range(4)
        for core in range(2)
        for at_y in range(4)
        for at_z in range(4)
    ]
    return lax.ppermute(block, AXES, pairs)


def peer_index(z_lo, x, core):
    return (z_lo * 4 + x) * 2 + core


def from_below(block):
    pairs = [(peer_index(z_lo, x, 1), peer_index(z_lo, (x + 1) % 4, 1)) for z_lo in range(2) for x in range(4)]
    return lax.ppermute(block, "peer", pairs)


def across(block):
    peers = lax.axis_size("peer")
    pairs = [(i, (i + HOP) % peers) for i in range(0, peers, 2)]
    pairs += [(peer_index(z_lo, (x + 1) % 4, 1), peer_index(z_lo, x, 1)) for z_lo in range(2) for x in range(4)]
    return lax.ppermute(block, "peer", pairs)


def swapped(block):
    pairs = [(peer_index(z_lo, 0, 1), peer_index(1 - z_lo, 0, 1)) for z_lo in range(2)]
    return lax.ppermute(block, "peer", pairs)


def contract_last(left, right):
    return lax.dot_general(
        left, right, (((1,), (1,)), ((), ())), preferred_element_type=jnp.float32
    )


def sub_blocks(piece):
    found = [()]
    for size in piece.shape[:-3]:
        found = [index + (i,) for index in found for i in range(size)]
    return found


def add_up(count, first, last, amount, pieces, weights, down, sum_in, outs, tokens, cots, slopes, sems):
    loads = []

    def begin(source, target):
        copy = pltpu.make_async_copy(source, target, sems.at[len(loads)])
        copy.start()
        loads.append(copy)

    offset = 0
    ends = []
    for piece in pieces:
        size = piece.shape[-2]
        for index in sub_blocks(piece):
            begin(piece.at[index + (0,)], tokens.at[pl.ds(offset, size)])
            begin(piece.at[index + (1,)], cots.at[pl.ds(offset, size)])
            offset += size
            ends += [offset, offset]
    padded = tokens.shape[0]
    if padded > offset:
        tokens[offset:, :] = jnp.zeros((padded - offset, D), jnp.bfloat16)
        cots[offset:, :] = jnp.zeros((padded - offset, D), jnp.bfloat16)

    waited = 0
    for start in range(0, padded, TILE):
        size = min(TILE, padded - start)
        while waited < len(loads) and (waited == 0 or ends[waited - 1] < start + size):
            loads[waited].wait()
            loads[waited + 1].wait()
            waited += 2
        rows = pl.ds(start, size)
        both = contract_last(weights[...], tokens[rows, :]) * D ** (-0.5)
        gate, up = both[:ROWS], both[ROWS:]
        dhidden = contract_last(down[...], cots[rows, :]) * FF ** (-0.5)
        sigma = jax.nn.sigmoid(gate)
        slopes[:ROWS, rows] = (dhidden * up * sigma * (1.0 + gate * (1.0 - sigma))).astype(
            jnp.bfloat16
        )
        slopes[ROWS:, rows] = (dhidden * gate * sigma).astype(jnp.bfloat16)

    for column in range(D // TILE):
        part = pl.ds(column * TILE, TILE)
        grad = jnp.dot(slopes[...], tokens[:, part], preferred_element_type=jnp.float32)
        if not first:
            grad = sum_in[:, part] + grad
        if last:
            stepped = (
                weights[:, part].astype(jnp.float32) - rate_value * (grad * D ** (-0.5))
            ).astype(jnp.bfloat16)
            outs[0][:, part] = stepped[:ROWS]
            outs[1][:, part] = stepped[ROWS:]
        else:
            outs[0][:, part] = grad


def grad_kernel(count, first, last, amount, *refs):
    pieces = refs[:count]
    weights, down = refs[count : count + 2]
    refs = refs[count + 2 :]
    sum_in = None
    if not first:
        sum_in, refs = refs[0], refs[1:]
    wide = 2 if last else 1
    outs, scratch = refs[:wide], refs[wide:]
    add_up(count, first, last, amount, pieces, weights, down, sum_in, outs, *scratch)


def add_grads(pieces, weights, down, so_far=None, last=False):
    amount = 0
    copies = 0
    for piece in pieces:
        blocks = len(sub_blocks(piece))
        amount += blocks * piece.shape[-2]
        copies += 2 * blocks
    padded = -(-amount // 128) * 128
    first = so_far is None
    operands = list(pieces) + [weights, down] + ([] if first else [so_far])
    whole = pl.BlockSpec(memory_space=pltpu.VMEM)
    anywhere = pl.BlockSpec(memory_space=pl.ANY)
    in_specs = [anywhere] * len(pieces) + [whole] * (len(operands) - len(pieces))
    if last:
        out_shape = (jax.ShapeDtypeStruct((ROWS, D), jnp.bfloat16),) * 2
        out_specs = (whole, whole)
    else:
        out_shape = jax.ShapeDtypeStruct((2 * ROWS, D), jnp.float32)
        out_specs = whole
    return pl.pallas_call(
        functools.partial(grad_kernel, len(pieces), first, last, amount),
        out_shape=out_shape,
        in_specs=in_specs,
        out_specs=out_specs,
        input_output_aliases={} if first or last else {len(operands) - 1: 0},
        scratch_shapes=[
            pltpu.VMEM((padded, D), jnp.bfloat16),
            pltpu.VMEM((padded, D), jnp.bfloat16),
            pltpu.VMEM((2 * ROWS, padded), jnp.bfloat16),
            pltpu.SemaphoreType.DMA((copies,)),
        ],
        compiler_params=pltpu.CompilerParams(vmem_limit_bytes=14 * 1024 * 1024),
        cost_estimate=pl.CostEstimate(
            flops=10 * amount * D * ROWS, bytes_accessed=amount * D, transcendentals=0
        ),
    )(*operands)


def averaged(mine, theirs):
    return ((mine.astype(jnp.float32) + theirs.astype(jnp.float32)) * 0.5).astype(jnp.bfloat16)


def body(tokens, gate_weight, up_weight, down_weight, cotangent):
    move = shifted
    hold = lax.optimization_barrier
    join = functools.partial(jnp.concatenate, axis=1)
    place = lax.axis_index("peer")
    moved = place % 2 == 1

    own = jnp.stack([tokens[0], cotangent[0]])
    own = jnp.where(moved, from_below(own), own)

    weights = jnp.concatenate([gate_weight[0], up_weight[0], down_weight[0]])
    own, weights = hold((own, weights))
    weights = jnp.where(moved, from_below(weights), weights)
    weights, down = weights[: 2 * ROWS], weights[2 * ROWS :]
    grads = functools.partial(add_grads, weights=weights, down=down)

    y_up, y_down = move(own, y=1), move(own, y=-1)
    along_z = own[:, :FIRST]
    z_up, z_down = move(along_z, z=1), move(along_z, z=-1)

    half = TOKENS // 2
    far_y = (move(y_up[:, :half], y=1), move(y_down[:, half:], y=-1))
    half = FIRST // 2
    far_z = (move(z_up[:, :half], z=1), move(z_down[:, half:], z=-1))
    *far_y, z_up, z_down = hold((*far_y, z_up, z_down))
    near = jnp.stack([z_up, z_down])
    row = [part[:, FIRST:] for part in (own, y_up, y_down)] + [far_y[1][:, FIRST - TOKENS // 2 :]]
    row = join(row)
    near, row = hold((near, row))
    near_up, near_down = move(near, y=1), move(near, y=-1)
    *far_z, row = hold((*far_z, row))
    row_up, row_down = move(row, z=1), move(row, z=-1)
    own, row = hold((own, row))
    total = grads([own, y_up, y_down, *far_y, near, *far_z])

    opposite = join(far_z)
    near_up, near_down, opposite, total = hold((near_up, near_down, opposite, total))
    opposite_up, opposite_down = move(opposite, y=1), move(opposite, y=-1)
    total = grads([near_up, near_down], so_far=total)
    opposite_up, opposite_down, row_up, row_down, total = hold(
        (opposite_up, opposite_down, row_up, row_down, total)
    )
    wide = row.shape[1] // 2
    last_up = move(join([near_up[0], opposite_up[:, :half]]), y=1)
    last_down = move(join([near_down[1], opposite_down[:, half:]]), y=-1)
    row_far = (move(row_up[:, :wide], z=1), move(row_down[:, wide:], z=-1))
    total = grads([opposite_up, opposite_down, row_up, row_down], so_far=total)
    gate, up = grads([last_up, last_down, *row_far], so_far=total, last=True)
    got_gate, got_up = across(gate), across(up)
    at_end = place % 8 == 1
    gate = jnp.where(at_end, swapped(gate), gate)
    up = jnp.where(at_end, swapped(up), up)
    return (averaged(gate, got_gate)[None], averaged(up, got_up)[None])


def solution(mesh):
    spec = P("peer", "fsdp", None)
    return jax.shard_map(
        body,
        mesh=mesh,
        in_specs=(spec,) * 5,
        out_specs=(spec, spec),
        check_vma=False,
    )
```

```python
import functools

import jax
import jax.numpy as jnp
from jax import lax
from jax.experimental import pallas as pl
from jax.experimental.pallas import tpu as pltpu
from jax.sharding import PartitionSpec as P

D = 2048
FF = 5632
HOP = 2
ROWS = 352
TOKENS = 128
FIRST = 96
TILE = 256

rate_value = 1.0

AXES = ("peer", "fsdp")


def device_index(z_lo, x, core, y, z_hi):
    return ((z_lo * 4 + x) * 2 + core) * 16 + y * 4 + z_hi


def shifted(block, y=0, z=0):
    pairs = [
        (
            device_index(z_lo, x, core, at_y, at_z),
            device_index(z_lo, x, core, (at_y + y) % 4, (at_z + z) % 4),
        )
        for z_lo in range(2)
        for x in range(4)
        for core in range(2)
        for at_y in range(4)
        for at_z in range(4)
    ]
    return lax.ppermute(block, AXES, pairs)


def peer_index(z_lo, x, core):
    return (z_lo * 4 + x) * 2 + core


def from_below(block):
    pairs = [(peer_index(z_lo, x, 1), peer_index(z_lo, (x + 1) % 4, 1)) for z_lo in range(2) for x in range(4)]
    return lax.ppermute(block, "peer", pairs)


def across(block):
    peers = lax.axis_size("peer")
    pairs = [(i, (i + HOP) % peers) for i in range(0, peers, 2)]
    pairs += [(peer_index(z_lo, (x + 1) % 4, 1), peer_index(z_lo, x, 1)) for z_lo in range(2) for x in range(4)]
    return lax.ppermute(block, "peer", pairs)


def swapped(block):
    pairs = [(peer_index(z_lo, 0, 1), peer_index(1 - z_lo, 0, 1)) for z_lo in range(2)]
    return lax.ppermute(block, "peer", pairs)


def contract_last(left, right):
    return lax.dot_general(
        left, right, (((1,), (1,)), ((), ())), preferred_element_type=jnp.float32
    )


def sub_blocks(piece):
    found = [()]
    for size in piece.shape[:-3]:
        found = [index + (i,) for index in found for i in range(size)]
    return found


def add_up(count, first, last, amount, pieces, weights, down, sum_in, outs, tokens, cots, slopes, sems):
    loads = []

    def begin(source, target):
        copy = pltpu.make_async_copy(source, target, sems.at[len(loads)])
        copy.start()
        loads.append(copy)

    offset = 0
    ends = []
    for piece in pieces:
        size = piece.shape[-2]
        for index in sub_blocks(piece):
            begin(piece.at[index + (0,)], tokens.at[pl.ds(offset, size)])
            begin(piece.at[index + (1,)], cots.at[pl.ds(offset, size)])
            offset += size
            ends += [offset, offset]
    padded = tokens.shape[0]
    if padded > offset:
        tokens[offset:, :] = jnp.zeros((padded - offset, D), jnp.bfloat16)
        cots[offset:, :] = jnp.zeros((padded - offset, D), jnp.bfloat16)

    waited = 0
    for start in range(0, padded, TILE):
        size = min(TILE, padded - start)
        while waited < len(loads) and (waited == 0 or ends[waited - 1] < start + size):
            loads[waited].wait()
            loads[waited + 1].wait()
            waited += 2
        rows = pl.ds(start, size)
        both = contract_last(weights[...], tokens[rows, :]) * D ** (-0.5)
        gate, up = both[:ROWS], both[ROWS:]
        dhidden = contract_last(down[...], cots[rows, :]) * FF ** (-0.5)
        sigma = jax.nn.sigmoid(gate)
        slopes[:ROWS, rows] = (dhidden * up * sigma * (1.0 + gate * (1.0 - sigma))).astype(
            jnp.bfloat16
        )
        slopes[ROWS:, rows] = (dhidden * gate * sigma).astype(jnp.bfloat16)

    for column in range(D // TILE):
        part = pl.ds(column * TILE, TILE)
        grad = jnp.dot(slopes[...], tokens[:, part], preferred_element_type=jnp.float32)
        if not first:
            grad = sum_in[:, part] + grad
        if last:
            stepped = (
                weights[:, part].astype(jnp.float32) - rate_value * (grad * D ** (-0.5))
            ).astype(jnp.bfloat16)
            outs[0][:, part] = stepped[:ROWS]
            outs[1][:, part] = stepped[ROWS:]
            outs[2][:, part] = stepped
        else:
            outs[0][:, part] = grad


def grad_kernel(count, first, last, amount, *refs):
    pieces = refs[:count]
    weights, down = refs[count : count + 2]
    refs = refs[count + 2 :]
    sum_in = None
    if not first:
        sum_in, refs = refs[0], refs[1:]
    wide = 3 if last else 1
    outs, scratch = refs[:wide], refs[wide:]
    add_up(count, first, last, amount, pieces, weights, down, sum_in, outs, *scratch)


def add_grads(pieces, weights, down, so_far=None, last=False):
    amount = 0
    copies = 0
    for piece in pieces:
        blocks = len(sub_blocks(piece))
        amount += blocks * piece.shape[-2]
        copies += 2 * blocks
    padded = -(-amount // 128) * 128
    first = so_far is None
    operands = list(pieces) + [weights, down] + ([] if first else [so_far])
    whole = pl.BlockSpec(memory_space=pltpu.VMEM)
    anywhere = pl.BlockSpec(memory_space=pl.ANY)
    in_specs = [anywhere] * len(pieces) + [whole] * (len(operands) - len(pieces))
    if last:
        out_shape = (jax.ShapeDtypeStruct((ROWS, D), jnp.bfloat16),) * 2
        out_shape += (jax.ShapeDtypeStruct((2 * ROWS, D), jnp.bfloat16),)
        out_specs = (whole,) * 3
    else:
        out_shape = jax.ShapeDtypeStruct((2 * ROWS, D), jnp.float32)
        out_specs = whole
    return pl.pallas_call(
        functools.partial(grad_kernel, len(pieces), first, last, amount),
        out_shape=out_shape,
        in_specs=in_specs,
        out_specs=out_specs,
        input_output_aliases={} if first or last else {len(operands) - 1: 0},
        scratch_shapes=[
            pltpu.VMEM((padded, D), jnp.bfloat16),
            pltpu.VMEM((padded, D), jnp.bfloat16),
            pltpu.VMEM((2 * ROWS, padded), jnp.bfloat16),
            pltpu.SemaphoreType.DMA((copies,)),
        ],
        compiler_params=pltpu.CompilerParams(vmem_limit_bytes=14 * 1024 * 1024),
        cost_estimate=pl.CostEstimate(
            flops=10 * amount * D * ROWS, bytes_accessed=amount * D, transcendentals=0
        ),
    )(*operands)


def averaged(mine, theirs):
    return ((mine.astype(jnp.float32) + theirs.astype(jnp.float32)) * 0.5).astype(jnp.bfloat16)


def body(tokens, gate_weight, up_weight, down_weight, cotangent):
    move = shifted
    hold = lax.optimization_barrier
    join = functools.partial(jnp.concatenate, axis=1)
    place = lax.axis_index("peer")
    moved = place % 2 == 1

    own = jnp.stack([tokens[0], cotangent[0]])
    own = jnp.where(moved, from_below(own), own)

    weights = jnp.concatenate([gate_weight[0], up_weight[0], down_weight[0]])
    own, weights = hold((own, weights))
    weights = jnp.where(moved, from_below(weights), weights)
    weights, down = weights[: 2 * ROWS], weights[2 * ROWS :]
    grads = functools.partial(add_grads, weights=weights, down=down)

    y_up, y_down = move(own, y=1), move(own, y=-1)
    along_z = own[:, :FIRST]
    z_up, z_down = move(along_z, z=1), move(along_z, z=-1)

    half = TOKENS // 2
    far_y = (move(y_up[:, :half], y=1), move(y_down[:, half:], y=-1))
    half = FIRST // 2
    far_z = (move(z_up[:, :half], z=1), move(z_down[:, half:], z=-1))
    *far_y, z_up, z_down = hold((*far_y, z_up, z_down))
    near = jnp.stack([z_up, z_down])
    row = [part[:, FIRST:] for part in (own, y_up, y_down)] + [far_y[1][:, FIRST - TOKENS // 2 :]]
    row = join(row)
    near, row = hold((near, row))
    near_up, near_down = move(near, y=1), move(near, y=-1)
    *far_z, row = hold((*far_z, row))
    row_up, row_down = move(row, z=1), move(row, z=-1)
    own, row = hold((own, row))
    total = grads([own, y_up, y_down, *far_y, near, *far_z])

    opposite = join(far_z)
    near_up, near_down, opposite, total = hold((near_up, near_down, opposite, total))
    opposite_up, opposite_down = move(opposite, y=1), move(opposite, y=-1)
    total = grads([near_up, near_down], so_far=total)
    opposite_up, opposite_down, row_up, row_down, total = hold(
        (opposite_up, opposite_down, row_up, row_down, total)
    )
    wide = row.shape[1] // 2
    last_up = move(join([near_up[0], opposite_up[:, :half]]), y=1)
    last_down = move(join([near_down[1], opposite_down[:, half:]]), y=-1)
    row_far = (move(row_up[:, :wide], z=1), move(row_down[:, wide:], z=-1))
    total = grads([opposite_up, opposite_down, row_up, row_down], so_far=total)
    at_end = place % 8 == 1
    gate, up, steps = grads([last_up, last_down, *row_far], so_far=total, last=True)
    got = across(steps)
    gate = jnp.where(at_end, swapped(gate), gate)
    up = jnp.where(at_end, swapped(up), up)
    gate, up = hold((gate, up))
    return (averaged(gate, got[:ROWS])[None], averaged(up, got[ROWS:])[None])


def solution(mesh):
    spec = P("peer", "fsdp", None)
    return jax.shard_map(
        body,
        mesh=mesh,
        in_specs=(spec,) * 5,
        out_specs=(spec, spec),
        check_vma=False,
    )
```

```python
import functools

import jax
import jax.numpy as jnp
from jax import lax
from jax.experimental import pallas as pl
from jax.experimental.pallas import tpu as pltpu
from jax.sharding import PartitionSpec as P

D = 2048
FF = 5632
HOP = 2
ROWS = 352
TOKENS = 128
FIRST = 96
TILE = 256

rate_value = 1.0

AXES = ("peer", "fsdp")


def device_index(z_lo, x, core, y, z_hi):
    return ((z_lo * 4 + x) * 2 + core) * 16 + y * 4 + z_hi


def shifted(block, y=0, z=0):
    pairs = [
        (
            device_index(z_lo, x, core, at_y, at_z),
            device_index(z_lo, x, core, (at_y + y) % 4, (at_z + z) % 4),
        )
        for z_lo in range(2)
        for x in range(4)
        for core in range(2)
        for at_y in range(4)
        for at_z in range(4)
    ]
    return lax.ppermute(block, AXES, pairs)


def peer_index(z_lo, x, core):
    return (z_lo * 4 + x) * 2 + core


def from_below(block):
    pairs = [(peer_index(z_lo, x, 1), peer_index(z_lo, (x + 1) % 4, 1)) for z_lo in range(2) for x in range(4)]
    return lax.ppermute(block, "peer", pairs)


def from_other_core(block):
    peers = lax.axis_size("peer")
    return lax.ppermute(block, "peer", [(i + 1, i) for i in range(0, peers, 2)])


def across(block):
    peers = lax.axis_size("peer")
    pairs = [(i, (i + HOP) % peers) for i in range(0, peers, 2)]
    pairs += [(peer_index(z_lo, (x + 1) % 4, 1), peer_index(z_lo, x, 1)) for z_lo in range(2) for x in range(4)]
    return lax.ppermute(block, "peer", pairs)


def swapped(block):
    pairs = [(peer_index(z_lo, 0, 1), peer_index(1 - z_lo, 0, 1)) for z_lo in range(2)]
    return lax.ppermute(block, "peer", pairs)


def contract_last(left, right):
    return lax.dot_general(
        left, right, (((1,), (1,)), ((), ())), preferred_element_type=jnp.float32
    )


def sub_blocks(piece):
    found = [()]
    for size in piece.shape[:-3]:
        found = [index + (i,) for index in found for i in range(size)]
    return found


def add_up(count, first, last, amount, pieces, weights, down, sum_in, outs, tokens, cots, slopes, sems):
    loads = []

    def begin(source, target):
        copy = pltpu.make_async_copy(source, target, sems.at[len(loads)])
        copy.start()
        loads.append(copy)

    offset = 0
    ends = []
    for piece in pieces:
        size = piece.shape[-2]
        for index in sub_blocks(piece):
            begin(piece.at[index + (0,)], tokens.at[pl.ds(offset, size)])
            begin(piece.at[index + (1,)], cots.at[pl.ds(offset, size)])
            offset += size
            ends += [offset, offset]
    padded = tokens.shape[0]
    if padded > offset:
        tokens[offset:, :] = jnp.zeros((padded - offset, D), jnp.bfloat16)
        cots[offset:, :] = jnp.zeros((padded - offset, D), jnp.bfloat16)

    waited = 0
    for start in range(0, padded, TILE):
        size = min(TILE, padded - start)
        while waited < len(loads) and (waited == 0 or ends[waited - 1] < start + size):
            loads[waited].wait()
            loads[waited + 1].wait()
            waited += 2
        rows = pl.ds(start, size)
        both = contract_last(weights[...], tokens[rows, :]) * D ** (-0.5)
        gate, up = both[:ROWS], both[ROWS:]
        dhidden = contract_last(down[...], cots[rows, :]) * FF ** (-0.5)
        sigma = jax.nn.sigmoid(gate)
        slopes[:ROWS, rows] = (dhidden * up * sigma * (1.0 + gate * (1.0 - sigma))).astype(
            jnp.bfloat16
        )
        slopes[ROWS:, rows] = (dhidden * gate * sigma).astype(jnp.bfloat16)

    for column in range(D // TILE):
        part = pl.ds(column * TILE, TILE)
        grad = jnp.dot(slopes[...], tokens[:, part], preferred_element_type=jnp.float32)
        if not first:
            grad = sum_in[:, part] + grad
        if last:
            stepped = (
                weights[:, part].astype(jnp.float32) - rate_value * (grad * D ** (-0.5))
            ).astype(jnp.bfloat16)
            outs[0][:, part] = stepped[:ROWS]
            outs[1][:, part] = stepped[ROWS:]
        else:
            outs[0][:, part] = grad


def grad_kernel(count, first, last, amount, *refs):
    pieces = refs[:count]
    weights, down = refs[count : count + 2]
    refs = refs[count + 2 :]
    sum_in = None
    if not first:
        sum_in, refs = refs[0], refs[1:]
    wide = 2 if last else 1
    outs, scratch = refs[:wide], refs[wide:]
    add_up(count, first, last, amount, pieces, weights, down, sum_in, outs, *scratch)


def add_grads(pieces, weights, down, so_far=None, last=False, part=10):
    amount = 0
    copies = 0
    for piece in pieces:
        blocks = len(sub_blocks(piece))
        amount += blocks * piece.shape[-2]
        copies += 2 * blocks
    padded = -(-amount // 128) * 128
    first = so_far is None
    operands = list(pieces) + [weights, down] + ([] if first else [so_far])
    whole = pl.BlockSpec(memory_space=pltpu.VMEM)
    anywhere = pl.BlockSpec(memory_space=pl.ANY)
    in_specs = [anywhere] * len(pieces) + [whole] * (len(operands) - len(pieces))
    if last:
        out_shape = (jax.ShapeDtypeStruct((ROWS, D), jnp.bfloat16),) * 2
        out_specs = (whole, whole)
    else:
        out_shape = jax.ShapeDtypeStruct((2 * ROWS, D), jnp.float32)
        out_specs = whole
    return pl.pallas_call(
        functools.partial(grad_kernel, len(pieces), first, last, amount),
        out_shape=out_shape,
        in_specs=in_specs,
        out_specs=out_specs,
        input_output_aliases={} if first or last else {len(operands) - 1: 0},
        scratch_shapes=[
            pltpu.VMEM((padded, D), jnp.bfloat16),
            pltpu.VMEM((padded, D), jnp.bfloat16),
            pltpu.VMEM((2 * ROWS, padded), jnp.bfloat16),
            pltpu.SemaphoreType.DMA((copies,)),
        ],
        compiler_params=pltpu.CompilerParams(vmem_limit_bytes=14 * 1024 * 1024),
        cost_estimate=pl.CostEstimate(
            flops=int(part * amount * D * ROWS), bytes_accessed=amount * D, transcendentals=0
        ),
    )(*operands)


def averaged(mine, theirs):
    return ((mine.astype(jnp.float32) + theirs.astype(jnp.float32)) * 0.5).astype(jnp.bfloat16)


def body(tokens, gate_weight, up_weight, down_weight, cotangent):
    move = shifted
    hold = lax.optimization_barrier
    join = functools.partial(jnp.concatenate, axis=1)
    place = lax.axis_index("peer")
    moved = place % 2 == 1

    own = jnp.stack([tokens[0], cotangent[0]])
    own = jnp.where(moved, from_below(own), own)

    weights = jnp.concatenate([gate_weight[0], up_weight[0], down_weight[0]])
    own, weights = hold((own, weights))
    weights = jnp.where(moved, from_below(weights), weights)
    weights, down = weights[: 2 * ROWS], weights[2 * ROWS :]
    grads = functools.partial(add_grads, weights=weights, down=down)

    y_up, y_down = move(own, y=1), move(own, y=-1)
    along_z = own[:, :FIRST]
    z_up, z_down = move(along_z, z=1), move(along_z, z=-1)

    half = TOKENS // 2
    far_y = (move(y_up[:, :half], y=1), move(y_down[:, half:], y=-1))
    half = FIRST // 2
    far_z = (move(z_up[:, :half], z=1), move(z_down[:, half:], z=-1))
    *far_y, z_up, z_down = hold((*far_y, z_up, z_down))
    near = jnp.stack([z_up, z_down])
    row = [part[:, FIRST:] for part in (own, y_up, y_down)] + [far_y[1][:, FIRST - TOKENS // 2 :]]
    row = join(row)
    near, row = hold((near, row))
    near_up, near_down = move(near, y=1), move(near, y=-1)
    *far_z, row = hold((*far_z, row))
    row, told = hold((row, from_other_core(far_z[0][0, :16] + far_z[1][0, :16])))
    row_up, row_down = move(row, z=1), move(row, z=-1)
    own, row = hold((own, row))
    total = grads([own, y_up, y_down, *far_y, near, *far_z], part=0.2)

    opposite = join(far_z)
    near_up, near_down, opposite, total = hold((near_up, near_down, opposite, total))
    opposite_up, opposite_down = move(opposite, y=1), move(opposite, y=-1)
    total = grads([near_up, near_down], so_far=total)
    opposite_up, opposite_down, row_up, row_down, total = hold(
        (opposite_up, opposite_down, row_up, row_down, total)
    )
    wide = row.shape[1] // 2
    last_up = move(join([near_up[0], opposite_up[:, :half]]), y=1)
    last_down = move(join([near_down[1], opposite_down[:, half:]]), y=-1)
    row_far = (move(row_up[:, :wide], z=1), move(row_down[:, wide:], z=-1))
    total = grads([opposite_up, opposite_down, row_up, row_down], so_far=total)
    gate, up = grads([last_up, last_down, *row_far], so_far=total, last=True)
    got_gate, got_up = across(gate), across(up)
    at_end = (place % 8 == 1) & (told[0, 0] < 128.0)
    gate = jnp.where(at_end, swapped(gate), gate)
    up = jnp.where(at_end, swapped(up), up)
    return (averaged(gate, got_gate)[None], averaged(up, got_up)[None])


def solution(mesh):
    spec = P("peer", "fsdp", None)
    return jax.shard_map(
        body,
        mesh=mesh,
        in_specs=(spec,) * 5,
        out_specs=(spec, spec),
        check_vma=False,
    )
```

```python
import functools

import jax
import jax.numpy as jnp
from jax import lax
from jax.experimental import pallas as pl
from jax.experimental.pallas import tpu as pltpu
from jax.sharding import PartitionSpec as P

D = 2048
FF = 5632
HOP = 2
ROWS = 352
TOKENS = 128
FIRST = 96
TILE = 256

rate_value = 1.0

AXES = ("peer", "fsdp")


def device_index(z_lo, x, core, y, z_hi):
    return ((z_lo * 4 + x) * 2 + core) * 16 + y * 4 + z_hi


def shifted(block, y=0, z=0):
    pairs = [
        (
            device_index(z_lo, x, core, at_y, at_z),
            device_index(z_lo, x, core, (at_y + y) % 4, (at_z + z) % 4),
        )
        for z_lo in range(2)
        for x in range(4)
        for core in range(2)
        for at_y in range(4)
        for at_z in range(4)
    ]
    return lax.ppermute(block, AXES, pairs)


def peer_index(z_lo, x, core):
    return (z_lo * 4 + x) * 2 + core


def from_below(block):
    pairs = [(peer_index(z_lo, x, 1), peer_index(z_lo, (x + 1) % 4, 1)) for z_lo in range(2) for x in range(4)]
    return lax.ppermute(block, "peer", pairs)


def across(block):
    peers = lax.axis_size("peer")
    pairs = [(i, (i + HOP) % peers) for i in range(0, peers, 2)]
    pairs += [(peer_index(z_lo, (x + 1) % 4, 1), peer_index(z_lo, x, 1)) for z_lo in range(2) for x in range(4)]
    return lax.ppermute(block, "peer", pairs)


def swapped(block):
    pairs = [(peer_index(z_lo, 0, 1), peer_index(1 - z_lo, 0, 1)) for z_lo in range(2)]
    return lax.ppermute(block, "peer", pairs)


def contract_last(left, right):
    return lax.dot_general(
        left, right, (((1,), (1,)), ((), ())), preferred_element_type=jnp.float32
    )


def sub_blocks(piece):
    found = [()]
    for size in piece.shape[:-3]:
        found = [index + (i,) for index in found for i in range(size)]
    return found


def add_up(count, first, last, amount, pieces, weights, down, sum_in, outs, tokens, cots, slopes, sems):
    loads = []

    def begin(source, target):
        copy = pltpu.make_async_copy(source, target, sems.at[len(loads)])
        copy.start()
        loads.append(copy)

    offset = 0
    ends = []
    for piece in pieces:
        size = piece.shape[-2]
        for index in sub_blocks(piece):
            begin(piece.at[index + (0,)], tokens.at[pl.ds(offset, size)])
            begin(piece.at[index + (1,)], cots.at[pl.ds(offset, size)])
            offset += size
            ends += [offset, offset]
    padded = tokens.shape[0]
    if padded > offset:
        tokens[offset:, :] = jnp.zeros((padded - offset, D), jnp.bfloat16)
        cots[offset:, :] = jnp.zeros((padded - offset, D), jnp.bfloat16)

    waited = 0
    for start in range(0, padded, TILE):
        size = min(TILE, padded - start)
        while waited < len(loads) and (waited == 0 or ends[waited - 1] < start + size):
            loads[waited].wait()
            loads[waited + 1].wait()
            waited += 2
        rows = pl.ds(start, size)
        both = contract_last(weights[...], tokens[rows, :]) * D ** (-0.5)
        gate, up = both[:ROWS], both[ROWS:]
        dhidden = contract_last(down[...], cots[rows, :]) * FF ** (-0.5)
        sigma = jax.nn.sigmoid(gate)
        slopes[:ROWS, rows] = (dhidden * up * sigma * (1.0 + gate * (1.0 - sigma))).astype(
            jnp.bfloat16
        )
        slopes[ROWS:, rows] = (dhidden * gate * sigma).astype(jnp.bfloat16)

    for column in range(D // TILE):
        part = pl.ds(column * TILE, TILE)
        grad = jnp.dot(slopes[...], tokens[:, part], preferred_element_type=jnp.float32)
        if not first:
            grad = sum_in[:, part] + grad
        if last:
            stepped = (
                weights[:, part].astype(jnp.float32) - rate_value * (grad * D ** (-0.5))
            ).astype(jnp.bfloat16)
            outs[0][:, part] = stepped[:ROWS]
            outs[1][:, part] = stepped[ROWS:]
        else:
            outs[0][:, part] = grad


def grad_kernel(count, first, last, amount, *refs):
    pieces = refs[:count]
    weights, down = refs[count : count + 2]
    refs = refs[count + 2 :]
    sum_in = None
    if not first:
        sum_in, refs = refs[0], refs[1:]
    wide = 2 if last else 1
    outs, scratch = refs[:wide], refs[wide:]
    add_up(count, first, last, amount, pieces, weights, down, sum_in, outs, *scratch)


def add_grads(pieces, weights, down, so_far=None, last=False):
    amount = 0
    copies = 0
    for piece in pieces:
        blocks = len(sub_blocks(piece))
        amount += blocks * piece.shape[-2]
        copies += 2 * blocks
    padded = -(-amount // 128) * 128
    first = so_far is None
    operands = list(pieces) + [weights, down] + ([] if first else [so_far])
    whole = pl.BlockSpec(memory_space=pltpu.VMEM)
    anywhere = pl.BlockSpec(memory_space=pl.ANY)
    in_specs = [anywhere] * len(pieces) + [whole] * (len(operands) - len(pieces))
    if last:
        out_shape = (jax.ShapeDtypeStruct((ROWS, D), jnp.bfloat16),) * 2
        out_specs = (whole, whole)
    else:
        out_shape = jax.ShapeDtypeStruct((2 * ROWS, D), jnp.float32)
        out_specs = whole
    return pl.pallas_call(
        functools.partial(grad_kernel, len(pieces), first, last, amount),
        out_shape=out_shape,
        in_specs=in_specs,
        out_specs=out_specs,
        input_output_aliases={} if first or last else {len(operands) - 1: 0},
        scratch_shapes=[
            pltpu.VMEM((padded, D), jnp.bfloat16),
            pltpu.VMEM((padded, D), jnp.bfloat16),
            pltpu.VMEM((2 * ROWS, padded), jnp.bfloat16),
            pltpu.SemaphoreType.DMA((copies,)),
        ],
        compiler_params=pltpu.CompilerParams(vmem_limit_bytes=14 * 1024 * 1024),
        cost_estimate=pl.CostEstimate(
            flops=10 * amount * D * ROWS, bytes_accessed=amount * D, transcendentals=0
        ),
    )(*operands)


def averaged(mine, theirs):
    return ((mine.astype(jnp.float32) + theirs.astype(jnp.float32)) * 0.5).astype(jnp.bfloat16)


def body(tokens, gate_weight, up_weight, down_weight, cotangent):
    move = shifted
    hold = lax.optimization_barrier
    join = functools.partial(jnp.concatenate, axis=1)
    place = lax.axis_index("peer")
    moved = place % 2 == 1

    own = jnp.stack([tokens[0], cotangent[0]])
    own = jnp.where(moved, from_below(own), own)

    y_up, y_down = move(own, y=1), move(own, y=-1)
    along_z = own[:, :FIRST]
    z_up, z_down = move(along_z, z=1), move(along_z, z=-1)

    half = TOKENS // 2
    y_up, y_down, *weights = hold((y_up, y_down, gate_weight[0], up_weight[0], down_weight[0]))
    far_y = (move(y_up[:, :half], y=1), move(y_down[:, half:], y=-1))
    weights = jnp.concatenate(weights)
    half = FIRST // 2
    far_z = (move(z_up[:, :half], z=1), move(z_down[:, half:], z=-1))
    *far_y, z_up, z_down, weights = hold((*far_y, z_up, z_down, weights))
    weights = jnp.where(moved, from_below(weights), weights)
    weights, down = weights[: 2 * ROWS], weights[2 * ROWS :]
    grads = functools.partial(add_grads, weights=weights, down=down)
    near = jnp.stack([z_up, z_down])
    row = [part[:, FIRST:] for part in (own, y_up, y_down)] + [far_y[1][:, FIRST - TOKENS // 2 :]]
    row = join(row)
    near_up, near_down = move(near, y=1), move(near, y=-1)
    *far_z, row = hold((*far_z, row))
    row_up, row_down = move(row, z=1), move(row, z=-1)
    own, row = hold((own, row))

    opposite = join(far_z)
    near_up, near_down, opposite = hold((near_up, near_down, opposite))
    opposite_up, opposite_down = move(opposite, y=1), move(opposite, y=-1)
    total = grads([own, y_up, y_down, *far_y, near, *far_z])
    opposite_up, opposite_down, row_up, row_down, total = hold(
        (opposite_up, opposite_down, row_up, row_down, total)
    )
    wide = row.shape[1] // 2
    last_up = move(join([near_up[0], opposite_up[:, :half]]), y=1)
    last_down = move(join([near_down[1], opposite_down[:, half:]]), y=-1)
    row_far = (move(row_up[:, :wide], z=1), move(row_down[:, wide:], z=-1))
    total = grads([near_up, near_down, opposite_up, opposite_down, row_up, row_down], so_far=total)
    gate, up = grads([last_up, last_down, *row_far], so_far=total, last=True)
    got_gate, got_up = across(gate), across(up)
    at_end = place % 8 == 1
    gate = jnp.where(at_end, swapped(gate), gate)
    up = jnp.where(at_end, swapped(up), up)
    return (averaged(gate, got_gate)[None], averaged(up, got_up)[None])


def solution(mesh):
    spec = P("peer", "fsdp", None)
    return jax.shard_map(
        body,
        mesh=mesh,
        in_specs=(spec,) * 5,
        out_specs=(spec, spec),
        check_vma=False,
    )
```

```python
import functools

import jax
import jax.numpy as jnp
from jax import lax
from jax.experimental import pallas as pl
from jax.experimental.pallas import tpu as pltpu
from jax.sharding import PartitionSpec as P

D = 2048
FF = 5632
HOP = 2
ROWS = 352
TOKENS = 128
FIRST = 96
TILE = 256

rate_value = 1.0

AXES = ("peer", "fsdp")


def device_index(z_lo, x, core, y, z_hi):
    return ((z_lo * 4 + x) * 2 + core) * 16 + y * 4 + z_hi


def shifted(block, y=0, z=0):
    pairs = [
        (
            device_index(z_lo, x, core, at_y, at_z),
            device_index(z_lo, x, core, (at_y + y) % 4, (at_z + z) % 4),
        )
        for z_lo in range(2)
        for x in range(4)
        for core in range(2)
        for at_y in range(4)
        for at_z in range(4)
    ]
    return lax.ppermute(block, AXES, pairs)


def peer_index(z_lo, x, core):
    return (z_lo * 4 + x) * 2 + core


def from_below(block):
    pairs = [(peer_index(z_lo, x, 1), peer_index(z_lo, (x + 1) % 4, 1)) for z_lo in range(2) for x in range(4)]
    return lax.ppermute(block, "peer", pairs)


def across(block):
    peers = lax.axis_size("peer")
    pairs = [(i, (i + HOP) % peers) for i in range(0, peers, 2)]
    pairs += [(peer_index(z_lo, (x + 1) % 4, 1), peer_index(z_lo, x, 1)) for z_lo in range(2) for x in range(4)]
    return lax.ppermute(block, "peer", pairs)


def swapped(block):
    pairs = [(peer_index(z_lo, 0, 1), peer_index(1 - z_lo, 0, 1)) for z_lo in range(2)]
    return lax.ppermute(block, "peer", pairs)


def contract_last(left, right):
    return lax.dot_general(
        left, right, (((1,), (1,)), ((), ())), preferred_element_type=jnp.float32
    )


def sub_blocks(piece):
    found = [()]
    for size in piece.shape[:-3]:
        found = [index + (i,) for index in found for i in range(size)]
    return found


def add_up(count, first, last, amount, pieces, weights, down, sum_in, outs, tokens, cots, slopes, sems):
    loads = []

    def begin(source, target):
        copy = pltpu.make_async_copy(source, target, sems.at[len(loads)])
        copy.start()
        loads.append(copy)

    offset = 0
    ends = []
    for piece in pieces:
        size = piece.shape[-2]
        for index in sub_blocks(piece):
            begin(piece.at[index + (0,)], tokens.at[pl.ds(offset, size)])
            begin(piece.at[index + (1,)], cots.at[pl.ds(offset, size)])
            offset += size
            ends += [offset, offset]
    padded = tokens.shape[0]
    if padded > offset:
        tokens[offset:, :] = jnp.zeros((padded - offset, D), jnp.bfloat16)
        cots[offset:, :] = jnp.zeros((padded - offset, D), jnp.bfloat16)

    waited = 0
    for start in range(0, padded, TILE):
        size = min(TILE, padded - start)
        while waited < len(loads) and (waited == 0 or ends[waited - 1] < start + size):
            loads[waited].wait()
            loads[waited + 1].wait()
            waited += 2
        rows = pl.ds(start, size)
        both = contract_last(weights[...], tokens[rows, :]) * D ** (-0.5)
        gate, up = both[:ROWS], both[ROWS:]
        dhidden = contract_last(down[...], cots[rows, :]) * FF ** (-0.5)
        sigma = jax.nn.sigmoid(gate)
        slopes[:ROWS, rows] = (dhidden * up * sigma * (1.0 + gate * (1.0 - sigma))).astype(
            jnp.bfloat16
        )
        slopes[ROWS:, rows] = (dhidden * gate * sigma).astype(jnp.bfloat16)

    for column in range(D // TILE):
        part = pl.ds(column * TILE, TILE)
        grad = jnp.dot(slopes[...], tokens[:, part], preferred_element_type=jnp.float32)
        if not first:
            grad = sum_in[:, part] + grad
        if last:
            stepped = (
                weights[:, part].astype(jnp.float32) - rate_value * (grad * D ** (-0.5))
            ).astype(jnp.bfloat16)
            outs[0][:, part] = stepped[:ROWS]
            outs[1][:, part] = stepped[ROWS:]
        else:
            outs[0][:, part] = grad


def grad_kernel(count, first, last, amount, *refs):
    pieces = refs[:count]
    weights, down = refs[count : count + 2]
    refs = refs[count + 2 :]
    sum_in = None
    if not first:
        sum_in, refs = refs[0], refs[1:]
    wide = 2 if last else 1
    outs, scratch = refs[:wide], refs[wide:]
    add_up(count, first, last, amount, pieces, weights, down, sum_in, outs, *scratch)


def add_grads(pieces, weights, down, so_far=None, last=False):
    amount = 0
    copies = 0
    for piece in pieces:
        blocks = len(sub_blocks(piece))
        amount += blocks * piece.shape[-2]
        copies += 2 * blocks
    padded = -(-amount // 128) * 128
    first = so_far is None
    operands = list(pieces) + [weights, down] + ([] if first else [so_far])
    whole = pl.BlockSpec(memory_space=pltpu.VMEM)
    anywhere = pl.BlockSpec(memory_space=pl.ANY)
    in_specs = [anywhere] * len(pieces) + [whole] * (len(operands) - len(pieces))
    if last:
        out_shape = (jax.ShapeDtypeStruct((ROWS, D), jnp.bfloat16),) * 2
        out_specs = (whole, whole)
    else:
        out_shape = jax.ShapeDtypeStruct((2 * ROWS, D), jnp.float32)
        out_specs = whole
    return pl.pallas_call(
        functools.partial(grad_kernel, len(pieces), first, last, amount),
        out_shape=out_shape,
        in_specs=in_specs,
        out_specs=out_specs,
        input_output_aliases={} if first or last else {len(operands) - 1: 0},
        scratch_shapes=[
            pltpu.VMEM((padded, D), jnp.bfloat16),
            pltpu.VMEM((padded, D), jnp.bfloat16),
            pltpu.VMEM((2 * ROWS, padded), jnp.bfloat16),
            pltpu.SemaphoreType.DMA((copies,)),
        ],
        compiler_params=pltpu.CompilerParams(vmem_limit_bytes=14 * 1024 * 1024),
        cost_estimate=pl.CostEstimate(
            flops=10 * amount * D * ROWS, bytes_accessed=amount * D, transcendentals=0
        ),
    )(*operands)


def averaged(mine, theirs):
    return ((mine.astype(jnp.float32) + theirs.astype(jnp.float32)) * 0.5).astype(jnp.bfloat16)


def body(tokens, gate_weight, up_weight, down_weight, cotangent):
    move = shifted
    hold = lax.optimization_barrier
    join = functools.partial(jnp.concatenate, axis=1)
    place = lax.axis_index("peer")
    moved = place % 2 == 1

    own = jnp.stack([tokens[0], cotangent[0]])
    own = jnp.where(moved, from_below(own), own)

    y_up, y_down = move(own, y=1), move(own, y=-1)
    along_z = own[:, :FIRST]
    z_up, z_down = move(along_z, z=1), move(along_z, z=-1)

    half = TOKENS // 2
    y_up, y_down, *weights = hold((y_up, y_down, gate_weight[0], up_weight[0], down_weight[0]))
    far_y = (move(y_up[:, :half], y=1), move(y_down[:, half:], y=-1))
    weights = jnp.concatenate(weights)
    half = FIRST // 2
    far_z = (move(z_up[:, :half], z=1), move(z_down[:, half:], z=-1))
    *far_y, z_up, z_down, weights = hold((*far_y, z_up, z_down, weights))
    weights = jnp.where(moved, from_below(weights), weights)
    weights, down = weights[: 2 * ROWS], weights[2 * ROWS :]
    grads = functools.partial(add_grads, weights=weights, down=down)
    near = jnp.stack([z_up, z_down])
    row = [part[:, FIRST:] for part in (own, y_up, y_down)] + [far_y[1][:, FIRST - TOKENS // 2 :]]
    row = join(row)
    near_up, near_down = move(near, y=1), move(near, y=-1)
    *far_z, row = hold((*far_z, row))
    row_up, row_down = move(row, z=1), move(row, z=-1)
    own, row = hold((own, row))

    opposite = join(far_z)
    near_up, near_down, opposite = hold((near_up, near_down, opposite))
    opposite_up, opposite_down = move(opposite, y=1), move(opposite, y=-1)
    total = grads([own, y_up, y_down, *far_y, near, far_z[0]])
    opposite_up, opposite_down, row_up, row_down, total = hold(
        (opposite_up, opposite_down, row_up, row_down, total)
    )
    wide = row.shape[1] // 2
    last_up = move(join([near_up[0], opposite_up[:, :half]]), y=1)
    last_down = move(join([near_down[1], opposite_down[:, half:]]), y=-1)
    row_far = (move(row_up[:, :wide], z=1), move(row_down[:, wide:], z=-1))
    total = grads(
        [far_z[1], near_up, near_down, opposite_up, opposite_down, row_up, row_down], so_far=total
    )
    gate, up = grads([last_up, last_down, *row_far], so_far=total, last=True)
    got_gate, got_up = across(gate), across(up)
    at_end = place % 8 == 1
    gate = jnp.where(at_end, swapped(gate), gate)
    up = jnp.where(at_end, swapped(up), up)
    return (averaged(gate, got_gate)[None], averaged(up, got_up)[None])


def solution(mesh):
    spec = P("peer", "fsdp", None)
    return jax.shard_map(
        body,
        mesh=mesh,
        in_specs=(spec,) * 5,
        out_specs=(spec, spec),
        check_vma=False,
    )
```
